32 devices in a mesh: row: 8 (over y, x, core), loop: 4 (over z).
Axes of the slice: x: 2, y: 2, z: 4, core: 2. Of those that a mesh axis runs over, the one named last changes fastest.
Arguments:
- features: bfloat16 [65536, 256], P(('row', 'loop')), may hold values from -6 to 6
- weight: bfloat16 [256, 256], replicated, may hold values from -0.375 to 0.375
- local_tiles: bfloat16 [4096, 128, 128], P(('row', 'loop')), may hold values from -0.1875 to 0.1875
- local_ids: int32 [4096], P(('row', 'loop')), may hold values from 0 to 255, as said below
- local_live: int32 [4096], P(('row', 'loop')), may hold values 0 or 1
- send_rows: int32 [32, 8, 256], P(('row', 'loop')), may hold values from 0 to 2047
- send_count: int32 [32, 8], P(('row', 'loop')), may hold values from 0 to 256, as said below
- edge_tiles: bfloat16 [4608, 128, 128], P(('row', 'loop')), may hold values from -0.25 to 0.25
- edge_ids: int32 [4608], P(('row', 'loop')), may hold values from 0 to 255, as said below
- edge_live: int32 [4608], P(('row', 'loop')), may hold values 0 or 1
- hub_feats: bfloat16 [1024, 256], P('loop'), may hold values from -6 to 6
- hub_adj: bfloat16 [65536, 1024], P(('row', 'loop')), may hold values from -0.25 to 0.25
- hub_live: int32 [512, 8], P(('row', 'loop')), may hold values 0 or 1
Outputs:
- layer_out: bfloat16 [65536, 256], P(('row', 'loop'))
The draws below stay inside these ranges and needn't reach their ends.
Inputs may be any that keep to these rules, and one draw needn't show every extreme that they name: `local_ids`: each entry is i * 16 + j, a tile of one block's 16 x 16 grid; the 128 entries of one device are distinct. `edge_ids`: each entry is i * 16 + j, a tile of a 16 x 16 grid; the 144 entries of one device are distinct. Only the first send_count[d, s] slots of send_rows[d, s] are sent with data. For every loop index, all devices of that loop index send 256 rows to one common row index.
All inputs are finite; a program needn't handle non-finite values. No bound on the sum of `local_live` or of `edge_live` or of `hub_live` on one device may be relied on, other than what follows from the above.
Results may differ from the reference program's by a relative error of at most 0.005.
Values may be sent and summed in bfloat16 or wider, within the bound.
No kernel may reach another device: no remote copies, remote signals or barrier semaphores. Data moves between devices by JAX's collectives and lax.ppermute only.
A program may use at most 256 MiB of HBM per device.

```python
import jax
import jax.numpy as jnp
from jax import lax

FEAT = 256
TILE = 128
ROWS_DEV = 2048
TILE_ROWS = 16
LOCAL_T = 128
SLOTS = 256
SLOT_TILES = 16
EDGE_T = 144
HUB = 1024
NODES = 65536
N_ROW = 8
N_LOOP = 4
DEVICES = 32


def draw_local_ids(key, part):
    key_list = jax.random.split(key, DEVICES)
    tile_grid = jax.vmap(lambda one_key: jax.random.permutation(one_key, TILE_ROWS * TILE_ROWS)[:LOCAL_T])(key_list)
    return tile_grid.reshape(DEVICES * LOCAL_T).astype(jnp.int32)


def draw_edge_ids(key, part):
    key_list = jax.random.split(jax.random.fold_in(key, 7), DEVICES)
    tile_grid = jax.vmap(lambda one_key: jax.random.permutation(one_key, TILE_ROWS * SLOT_TILES)[:EDGE_T])(key_list)
    return tile_grid.reshape(DEVICES * EDGE_T).astype(jnp.int32)


def draw_send_count(key, part):
    first_key = jax.random.fold_in(key, 11)
    second_key = jax.random.fold_in(key, 13)
    base_count = jax.random.randint(first_key, (DEVICES, N_ROW), 0, SLOTS + 1)
    hot_peer = jax.random.randint(second_key, (N_LOOP,), 0, N_ROW)
    loop_index = jnp.arange(DEVICES) % N_LOOP
    full_mask = hot_peer[loop_index][:, None] == jnp.arange(N_ROW)[None, :]
    return jnp.where(full_mask, SLOTS, base_count).astype(jnp.int32)


def set_ends(drawn, own_key, low, largest):
    shape = drawn.shape
    spot = [jax.random.randint(jax.random.fold_in(own_key, axis), (), 0, shape[axis]) for axis in range(len(shape))]
    drawn = drawn.at[tuple(spot)].set(low)
    longest = shape.index(max(shape))
    spot[longest] = (spot[longest] + 1) % shape[longest]
    return drawn.at[tuple(spot)].set(largest)


def steps_of(rng, extent, shards, least, top_value):
    loudness = 1.0
    for dim, blocks in shards:
        steps = jax.random.uniform(jax.random.fold_in(jax.random.fold_in(rng, 6), dim), (blocks,), jnp.float32, least / len(shards), top_value / len(shards))
        loudness = loudness * jnp.repeat(jnp.exp(steps), extent[dim] // blocks).reshape((-1,) + (1,) * (len(extent) - 1 - dim))
    return loudness


def normal_values(rng, extent, width, bound, cuts=(), kind=jnp.bfloat16):
    drawn = jax.random.normal(rng, extent, jnp.float32) * width
    if len(cuts) > 0:
        drawn = steps_of(rng, extent, cuts, -0.22, 0.18) * drawn
    return jnp.clip(drawn, min=-bound, max=bound).astype(kind)


def setup_inputs(seed: int = 0) -> dict:
    key_of = jax.random.split(jax.random.key(seed), 14)
    return {
        "features": normal_values(key_of[0], (NODES, FEAT), 1.0, 6.0, ((0, 32),)),
        "weight": normal_values(key_of[1], (FEAT, FEAT), FEAT ** -0.5, 0.375),
        "local_tiles": normal_values(key_of[2], (DEVICES * LOCAL_T, TILE, TILE), (ROWS_DEV // 2) ** -0.5, 0.1875, ((0, 32),)),
        "local_ids": draw_local_ids(jax.random.fold_in(key_of[13], 71), 0),
        "local_live": set_ends((jax.random.randint(key_of[4], (DEVICES * LOCAL_T,), 0, 4) < 3).astype(jnp.int32), jax.random.fold_in(key_of[4], 1), 0, 1),
        "send_rows": set_ends(jax.random.randint(key_of[5], (DEVICES, N_ROW, SLOTS), 0, ROWS_DEV), jax.random.fold_in(key_of[5], 1), 0, ROWS_DEV - 1).astype(jnp.int32),
        "send_count": draw_send_count(jax.random.fold_in(key_of[13], 71), 0),
        "edge_tiles": normal_values(key_of[7], (DEVICES * EDGE_T, TILE, TILE), (N_ROW * SLOTS // 4) ** -0.5, 0.25, ((0, 32),)),
        "edge_ids": draw_edge_ids(jax.random.fold_in(key_of[13], 71), 0),
        "edge_live": set_ends((jax.random.randint(key_of[9], (DEVICES * EDGE_T,), 0, 4) < 3).astype(jnp.int32), jax.random.fold_in(key_of[9], 1), 0, 1),
        "hub_feats": normal_values(key_of[10], (HUB, FEAT), 1.0, 6.0, ((0, 4),)),
        "hub_adj": normal_values(key_of[11], (NODES, HUB), (HUB // 2) ** -0.5, 0.25, ((0, 32),)),
        "hub_live": set_ends((jax.random.randint(key_of[12], (NODES // TILE, HUB // TILE), 0, 2) < 1).astype(jnp.int32), jax.random.fold_in(key_of[12], 1), 0, 1),
    }


def tile_term(tile_set, tile_ids, tile_live, panels, out_tiles, in_tiles):
    panel_grid = panels.reshape(in_tiles, TILE, FEAT)
    gathered = panel_grid[tile_ids % in_tiles]
    products = jnp.einsum("tab,tbf->taf", tile_set.astype(jnp.float32), gathered.astype(jnp.float32))
    row_select = (tile_ids // in_tiles)[:, None] == jnp.arange(out_tiles)[None, :]
    row_select = row_select.astype(jnp.float32) * tile_live[:, None].astype(jnp.float32)
    summed = jnp.einsum("tn,taf->naf", row_select, products, precision=lax.Precision.HIGHEST)
    return summed.reshape(out_tiles * TILE, FEAT)


def reference(features, weight, local_tiles, local_ids, local_live, send_rows, send_count, edge_tiles, edge_ids, edge_live, hub_feats, hub_adj, hub_live):
    devices = N_ROW * N_LOOP
    row_tiles = ROWS_DEV // TILE
    slot_cols = N_ROW * SLOTS // TILE
    blocks = features.reshape(devices, ROWS_DEV, FEAT)
    picked = jax.vmap(lambda block_rows, row_ids: block_rows[row_ids])(blocks, send_rows)
    kept_mask = jnp.arange(SLOTS)[None, None, :] < send_count[:, :, None]
    picked = jnp.where(kept_mask[..., None], picked, jnp.zeros((), jnp.bfloat16))
    received = picked.reshape(N_ROW, N_LOOP, N_ROW, SLOTS, FEAT).transpose(2, 1, 0, 3, 4).reshape(devices, N_ROW * SLOTS, FEAT)

    def one_block(inputs):
        block_feats, loc_set, loc_ids, loc_live, edg_set, edg_ids, edg_live, recv_rows, adj_rows, live_rows = inputs
        local_sum = tile_term(loc_set, loc_ids, loc_live, block_feats, row_tiles, row_tiles)
        edge_sum = tile_term(edg_set, edg_ids, edg_live, recv_rows, row_tiles, slot_cols)
        hub_mask = jnp.repeat(jnp.repeat(live_rows, TILE, 0), TILE, 1).astype(jnp.bfloat16)
        hub_sum = jnp.dot(adj_rows * hub_mask, hub_feats, preferred_element_type=jnp.float32)
        aggregated = (local_sum + edge_sum + hub_sum).astype(jnp.bfloat16)
        return jax.nn.relu(jnp.dot(aggregated, weight, preferred_element_type=jnp.float32)).astype(jnp.bfloat16)

    layer_out = lax.map(one_block, (
        blocks,
        local_tiles.reshape(devices, LOCAL_T, TILE, TILE),
        local_ids.reshape(devices, LOCAL_T),
        local_live.reshape(devices, LOCAL_T),
        edge_tiles.reshape(devices, EDGE_T, TILE, TILE),
        edge_ids.reshape(devices, EDGE_T),
        edge_live.reshape(devices, EDGE_T),
        received,
        hub_adj.reshape(devices, ROWS_DEV, HUB),
        hub_live.reshape(devices, row_tiles, HUB // TILE),
    ))
    return layer_out.reshape(devices * ROWS_DEV, FEAT)
```

```python
import functools

import jax
import jax.numpy as jnp
from jax import lax
from jax.experimental import pallas as pl
from jax.experimental.pallas import tpu as pltpu
from jax.sharding import PartitionSpec as P

BF = jnp.bfloat16
F32 = jnp.float32
I32 = jnp.int32
VMEM = pl.BlockSpec(memory_space=pltpu.VMEM)
SMEM = pl.BlockSpec(memory_space=pltpu.SMEM)
HBM = pl.BlockSpec(memory_space=pl.ANY)
MIB = 1 << 20


def params(mib):
    return pltpu.CompilerParams(vmem_limit_bytes=mib * MIB)


def dot(a, b):
    return jnp.dot(a, b, preferred_element_type=F32)


def gather_rows(send_ref, count_ref, feat_ref, peer):
    slots = send_ref.shape[1]
    rows = feat_ref.shape[0]
    index = send_ref[pl.ds(peer, 1), :]
    slot = lax.broadcasted_iota(I32, (1, slots), 1)
    index = jnp.where(slot < count_ref[0, peer], index, -1)
    lane = lax.broadcasted_iota(I32, (128, 128), 1)
    picks = []
    for part in range(slots // 128):
        column = jnp.broadcast_to(index[:, part * 128 : (part + 1) * 128], (128, 128)).T
        picks.append(
            jnp.concatenate(
                [jnp.where(column == lane + c * 128, 1.0, 0.0).astype(BF) for c in range(rows // 128)], axis=1
            )
        )
    return dot(jnp.concatenate(picks, axis=0), feat_ref[...]).astype(BF)


def pack_kernel(offsets, send_ref, count_ref, feat_ref, *out_refs):
    me = lax.axis_index("row")
    slots = send_ref.shape[1]
    for out_ref, group in zip(out_refs, offsets):
        for n, offset in enumerate(group):
            out_ref[n * slots : (n + 1) * slots, :] = gather_rows(send_ref, count_ref, feat_ref, me ^ offset)


def pack(offsets, send_rows, send_count, features):
    slots, width = send_rows.shape[1], features.shape[1]
    return pl.pallas_call(
        functools.partial(pack_kernel, offsets),
        out_shape=[jax.ShapeDtypeStruct((len(group) * slots, width), BF) for group in offsets],
        in_specs=[VMEM, SMEM, VMEM],
        out_specs=[VMEM] * len(offsets),
        compiler_params=params(16),
        name="pack",
    )(send_rows, send_count, features)


def fill_map(ids_ref, live_ref, map_ref):
    for cell in range(map_ref.shape[0]):
        map_ref[cell] = -1
    for t in range(ids_ref.shape[0]):
        map_ref[ids_ref[t]] = jnp.where(live_ref[t] > 0, t, -1)


def cell_tile(tiles_ref, map_ref, cell):
    slot = map_ref[cell]
    tile = tiles_ref[jnp.maximum(slot, 0)]
    return jnp.where(slot >= 0, tile, jnp.zeros_like(tile))


def local_kernel(block, ids_ref, live_ref, tiles_ref, feat_ref, out_ref, map_ref):
    fill_map(ids_ref, live_ref, map_ref)
    size = tiles_ref.shape[1]
    cols = feat_ref.shape[0] // size

    def body(m, _):
        rows = [
            jnp.concatenate([cell_tile(tiles_ref, map_ref, (m * block + i) * cols + j) for j in range(cols)], axis=1)
            for i in range(block)
        ]
        start = pl.multiple_of(m * block * size, block * size)
        out_ref[pl.ds(start, block * size), :] = dot(jnp.concatenate(rows, axis=0), feat_ref[...])
        return 0

    lax.fori_loop(0, out_ref.shape[0] // (block * size), body, 0)


def local_term(ids, live, tiles, features):
    return pl.pallas_call(
        functools.partial(local_kernel, 4),
        out_shape=jax.ShapeDtypeStruct(features.shape, F32),
        in_specs=[SMEM, SMEM, VMEM, VMEM],
        out_specs=VMEM,
        scratch_shapes=[pltpu.SMEM(((features.shape[0] // tiles.shape[1]) ** 2,), I32)],
        compiler_params=params(16),
        name="local",
    )(ids, live, tiles, features)


def edge_kernel(block, pieces, late, hubs, counts, *refs):
    ids_ref, live_ref, hub_live_ref, tiles_ref, adj_ref, acc_ref = refs[:6]
    array_refs = refs[6 : 6 + counts]
    out_ref, late_ref, map_ref, rhs_ref = refs[6 + counts :]
    me, loop = lax.axis_index("row"), lax.axis_index("loop")
    core = lax.rem(me, 2)
    size = tiles_ref.shape[1]
    rows, depth = adj_ref.shape
    cols = map_ref.shape[0] // (rows // size)
    slots = late_ref.shape[1] // len(late)
    per = slots // size
    fill_map(ids_ref, live_ref, map_ref)
    for array, first, count, offset, half in hubs:
        if half is None:
            start = pl.multiple_of((loop ^ offset) * count, count)
        else:
            start = pl.multiple_of((loop ^ offset) * 2 * count + (core ^ half) * count, count)
        rhs_ref[pl.ds(start, count), :] = array_refs[array][first : first + count, :]
    for n, (array, first, offset) in enumerate(pieces):
        rhs_ref[depth + n * slots : depth + (n + 1) * slots, :] = array_refs[array][first : first + slots, :]

    def body(m, _):
        blocks = []
        for i in range(block):
            row = m * block + i
            start = pl.multiple_of(row * size, size)
            line = []
            for b in range(depth // size):
                cell = adj_ref[pl.ds(start, size), b * size : (b + 1) * size]
                line.append(jnp.where(hub_live_ref[row, b] > 0, cell, jnp.zeros_like(cell)))
            for array, first, offset in pieces:
                for j in range(per):
                    line.append(cell_tile(tiles_ref, map_ref, row * cols + (me ^ offset) * per + j))
            blocks.append(jnp.concatenate(line, axis=1))
            for n, offset in enumerate(late):
                for j in range(per):
                    at = n * slots + j * size
                    late_ref[pl.ds(start, size), at : at + size] = cell_tile(
                        tiles_ref, map_ref, row * cols + (me ^ offset) * per + j
                    )
        span = pl.ds(pl.multiple_of(m * block * size, block * size), block * size)
        out_ref[span, :] = acc_ref[span, :] + dot(jnp.concatenate(blocks, axis=0), rhs_ref[...])
        return 0

    lax.fori_loop(0, rows // (block * size), body, 0)


def edge_term(pieces, late, hubs, slots, ids, live, hub_live, tiles, adj, acc, arrays):
    rows, depth = adj.shape
    size = tiles.shape[1]
    cells = (rows // size) * (lax.axis_size("row") * slots // size)
    return pl.pallas_call(
        functools.partial(edge_kernel, 4, pieces, late, hubs, len(arrays)),
        out_shape=[jax.ShapeDtypeStruct(acc.shape, F32), jax.ShapeDtypeStruct((rows, len(late) * slots), BF)],
        in_specs=[SMEM, SMEM, SMEM, VMEM, VMEM, VMEM] + [VMEM] * len(arrays),
        out_specs=[VMEM, VMEM],
        scratch_shapes=[pltpu.SMEM((cells,), I32), pltpu.VMEM((depth + len(pieces) * slots, acc.shape[1]), BF)],
        compiler_params=params(48),
        name="edge",
    )(ids, live, hub_live, tiles, adj, acc, *arrays)


def last_kernel(block, counts, acc_ref, late_ref, weight_ref, *refs):
    array_refs = refs[:counts]
    out_ref, stage_ref, sems = refs[counts:]
    depth = array_refs[0].shape[0]
    for m in range(acc_ref.shape[0] // block):
        span = slice(m * block, (m + 1) * block)
        total = acc_ref[span, :]
        for n in range(counts):
            total += dot(late_ref[span, n * depth : (n + 1) * depth], array_refs[n][...])
        stage_ref[span, :] = jnp.maximum(dot(total.astype(BF), weight_ref[...]), 0.0).astype(BF)
        pltpu.make_async_copy(stage_ref.at[span], out_ref.at[span], sems.at[m]).start()
    for m in range(acc_ref.shape[0] // block):
        span = slice(m * block, (m + 1) * block)
        pltpu.make_async_copy(stage_ref.at[span], out_ref.at[span], sems.at[m]).wait()


def last_term(acc, late, weight, arrays):
    block = 512
    return pl.pallas_call(
        functools.partial(last_kernel, block, len(arrays)),
        out_shape=jax.ShapeDtypeStruct(acc.shape, BF),
        in_specs=[VMEM] * (3 + len(arrays)),
        out_specs=HBM,
        scratch_shapes=[pltpu.VMEM(acc.shape, BF), pltpu.SemaphoreType.DMA((acc.shape[0] // block,))],
        compiler_params=params(32),
        name="last",
    )(acc, late, weight, *arrays)


def swap(x, axis, offset):
    return lax.ppermute(x, axis, [(i, i ^ offset) for i in range(lax.axis_size(axis))])


def join_kernel(offset_count, send_ref, count_ref, feat_ref, relayed_ref, *out_refs):
    me = lax.axis_index("row")
    slots = send_ref.shape[1]
    own_ref = out_refs[-1]
    for n, offset in enumerate(offset_count):
        out_refs[n][:slots, :] = gather_rows(send_ref, count_ref, feat_ref, me ^ offset)
        out_refs[n][slots:, :] = relayed_ref[n * slots : (n + 1) * slots, :]
    own_ref[...] = gather_rows(send_ref, count_ref, feat_ref, me)


def join(offsets, send_rows, send_count, features, relayed):
    slots, width = send_rows.shape[1], features.shape[1]
    return pl.pallas_call(
        functools.partial(join_kernel, offsets),
        out_shape=[jax.ShapeDtypeStruct((2 * slots, width), BF) for _ in offsets]
        + [jax.ShapeDtypeStruct((slots, width), BF)],
        in_specs=[VMEM, SMEM, VMEM, VMEM],
        out_specs=[VMEM] * (len(offsets) + 1),
        compiler_params=params(16),
        name="join",
    )(send_rows, send_count, features, relayed)


def per_device(
    features,
    weight,
    local_tiles,
    local_ids,
    local_live,
    send_rows,
    send_count,
    edge_tiles,
    edge_ids,
    edge_live,
    hub_feats,
    hub_adj,
    hub_live,
):
    peers, ring = lax.axis_size("row"), lax.axis_size("loop")
    slots = send_rows.shape[2]
    rows = send_rows[0]
    chips = range(2, peers, 2)
    early = [c for c in chips if c & (c - 1) == 0]
    late = [c for c in chips if c & (c - 1) != 0]
    first = pack([(c, c ^ 1) for c in early], rows, send_count, features)
    from_early = [swap(x, "row", c) for x, c in zip(first, early)]
    (relay,) = pack([tuple(c ^ 1 for c in late) + (1,)], rows, send_count, features)
    relayed = swap(relay, "row", 1)
    *second, own = join(late, rows, send_count, features, relayed)
    from_late = [swap(x, "row", c) for x, c in zip(second, late)]
    shared = [swap(x, "row", 1) for x in from_early]
    shard = hub_feats.shape[0]
    half = shard // 2
    core = lax.rem(lax.axis_index("row"), 2)
    mine = lax.dynamic_slice(hub_feats, (core * half, 0), (half, hub_feats.shape[1]))
    arrays = [hub_feats, swap(hub_feats, "loop", 1)]
    hubs = [(0, 0, shard, 0, None), (1, 0, shard, 1, None)]
    for offset in range(2, ring):
        got = swap(mine, "loop", offset)
        hubs += [(len(arrays), 0, half, offset, 0), (len(arrays) + 1, 0, half, offset, 1)]
        arrays += [got, swap(got, "row", 1)]
    pieces = [(len(arrays), 0, 0), (len(arrays) + 1, len(late) * slots, 1)]
    arrays += [own, relayed]
    for c, x, y in zip(early, from_early, shared):
        pieces += [(len(arrays), 0, c), (len(arrays) + 1, slots, c ^ 1)]
        arrays += [x, y]
    acc = local_term(local_ids, local_live, local_tiles, features)
    order = [c ^ core_bit for c in late for core_bit in (0, 1)]
    acc, late_tiles = edge_term(
        pieces, order, hubs, slots, edge_ids, edge_live, hub_live, edge_tiles, hub_adj, acc, arrays
    )
    return last_term(acc, late_tiles, weight, from_late)


def solution(mesh):
    both = ("row", "loop")
    placed = (
        P(both, None),
        P(),
        P(both, None, None),
        P(both),
        P(both),
        P(both, None, None),
        P(both, None),
        P(both, None, None),
        P(both),
        P(both),
        P("loop", None),
        P(both, None),
        P(both, None),
    )
    return jax.shard_map(per_device, mesh=mesh, in_specs=placed, out_specs=P(both, None), check_vma=False)
```

```python
import functools

import jax
import jax.numpy as jnp
from jax import lax
from jax.experimental import pallas as pl
from jax.experimental.pallas import tpu as pltpu
from jax.sharding import PartitionSpec as P

BF = jnp.bfloat16
F32 = jnp.float32
I32 = jnp.int32
VMEM = pl.BlockSpec(memory_space=pltpu.VMEM)
SMEM = pl.BlockSpec(memory_space=pltpu.SMEM)
HBM = pl.BlockSpec(memory_space=pltpu.HBM)
MIB = 1 << 20


def params(mib):
    return pltpu.CompilerParams(vmem_limit_bytes=mib * MIB)


def hbm(*arrays):
    return [pltpu.with_memory_space_constraint(x, pltpu.HBM) for x in arrays]


def dot(a, b):
    return jnp.dot(a, b, preferred_element_type=F32)


def gather_rows(send_ref, count_ref, feat_ref, peer):
    slots = send_ref.shape[1]
    rows = feat_ref.shape[0]
    index = send_ref[pl.ds(peer, 1), :]
    slot = lax.broadcasted_iota(I32, (1, slots), 1)
    index = jnp.where(slot < count_ref[0, peer], index, -1)
    lane = lax.broadcasted_iota(I32, (128, 128), 1)
    picks = []
    for part in range(slots // 128):
        column = jnp.broadcast_to(index[:, part * 128 : (part + 1) * 128], (128, 128)).T
        picks.append(
            jnp.concatenate(
                [jnp.where(column == lane + c * 128, 1.0, 0.0).astype(BF) for c in range(rows // 128)], axis=1
            )
        )
    return dot(jnp.concatenate(picks, axis=0), feat_ref[...]).astype(BF)


def pack_kernel(offsets, *refs):
    send_hbm, count_hbm, feat_hbm, hub_hbm, tiles_hbm = refs[:5]
    table_hbm = refs[5:10]
    feat_ref, hub_ref, tiles_ref, local_map, edge_map, hub_live_ref = refs[10:16]
    packed = refs[16 : 16 + len(offsets)]
    send_ref, count_ref, *tables, sems = refs[16 + len(offsets) :]
    local_ids, local_live, edge_ids, edge_live = tables
    copies = [
        pltpu.make_async_copy(source, target, sems.at[n])
        for n, (source, target) in enumerate(
            [
                (feat_hbm, feat_ref),
                (send_hbm, send_ref),
                (count_hbm, count_ref),
                (hub_hbm, hub_ref),
                *zip(table_hbm, (local_ids, local_live, edge_ids, edge_live, hub_live_ref)),
                (tiles_hbm, tiles_ref),
            ]
        )
    ]
    for copy in copies[:-1]:
        copy.start()
    for copy in copies[:-1]:
        copy.wait()
    copies[-1].start()
    me = lax.axis_index("row")
    slots = send_ref.shape[1]
    for n, group in enumerate(offsets):
        for k, offset in enumerate(group):
            packed[n][k * slots : (k + 1) * slots, :] = gather_rows(send_ref, count_ref, feat_ref, me ^ offset)
    fill_map(local_ids, local_live, local_map)
    fill_map(edge_ids, edge_live, edge_map)
    copies[-1].wait()


def pack(offsets, send_rows, send_count, features, hub_feats, local_tiles, tables, cells):
    slots, width = send_rows.shape[1], features.shape[1]
    total = sum(len(group) for group in offsets) * slots
    local_cells, edge_cells = cells
    return pl.pallas_call(
        functools.partial(pack_kernel, offsets),
        out_shape=[
            jax.ShapeDtypeStruct(features.shape, BF),
            jax.ShapeDtypeStruct(hub_feats.shape, BF),
            jax.ShapeDtypeStruct(local_tiles.shape, BF),
            jax.ShapeDtypeStruct((local_cells,), I32),
            jax.ShapeDtypeStruct((edge_cells,), I32),
            jax.ShapeDtypeStruct(tables[-1].shape, I32),
        ]
        + [jax.ShapeDtypeStruct((len(group) * slots, width), BF) for group in offsets],
        in_specs=[HBM] * 10,
        out_specs=[VMEM, VMEM, VMEM, SMEM, SMEM, SMEM] + [VMEM] * len(offsets),
        scratch_shapes=[pltpu.VMEM(send_rows.shape, I32), pltpu.SMEM(send_count.shape, I32)]
        + [pltpu.SMEM(table.shape, I32) for table in tables[:-1]]
        + [pltpu.SemaphoreType.DMA((10,))],
        compiler_params=params(16),
        cost_estimate=pl.CostEstimate(flops=0, bytes_accessed=0, transcendentals=0),
        name="pack",
    )(*hbm(send_rows, send_count, features, hub_feats, local_tiles, *tables))


def fill_map(ids_ref, live_ref, map_ref):
    for cell in range(map_ref.shape[0]):
        map_ref[cell] = -1
    for t in range(ids_ref.shape[0]):
        map_ref[ids_ref[t]] = jnp.where(live_ref[t] > 0, t, -1)


def cell_tile(tiles_ref, map_ref, cell):
    slot = map_ref[cell]
    tile = tiles_ref[jnp.maximum(slot, 0)]
    return jnp.where(slot >= 0, tile, jnp.zeros_like(tile))


def local_kernel(block, map_ref, tiles_ref, feat_ref, edge_hbm, adj_hbm, out_ref, edge_ref, adj_ref, sems):
    copies = [
        pltpu.make_async_copy(adj_hbm, adj_ref, sems.at[0]),
        pltpu.make_async_copy(edge_hbm, edge_ref, sems.at[1]),
    ]
    for copy in copies:
        copy.start()
    size = tiles_ref.shape[1]
    cols = feat_ref.shape[0] // size

    def body(m, _):
        rows = [
            jnp.concatenate([cell_tile(tiles_ref, map_ref, (m * block + i) * cols + j) for j in range(cols)], axis=1)
            for i in range(block)
        ]
        start = pl.multiple_of(m * block * size, block * size)
        out_ref[pl.ds(start, block * size), :] = dot(jnp.concatenate(rows, axis=0), feat_ref[...])
        return 0

    lax.fori_loop(0, out_ref.shape[0] // (block * size), body, 0)
    for copy in copies:
        copy.wait()


def local_term(local_map, tiles, features, edge_tiles, adj):
    return pl.pallas_call(
        functools.partial(local_kernel, 4),
        out_shape=[
            jax.ShapeDtypeStruct(features.shape, F32),
            jax.ShapeDtypeStruct(edge_tiles.shape, BF),
            jax.ShapeDtypeStruct(adj.shape, BF),
        ],
        in_specs=[SMEM, VMEM, VMEM, HBM, HBM],
        out_specs=[VMEM] * 3,
        scratch_shapes=[pltpu.SemaphoreType.DMA((2,))],
        compiler_params=params(16),
        cost_estimate=pl.CostEstimate(flops=0, bytes_accessed=0, transcendentals=0),
        name="local",
    )(local_map, tiles, features, *hbm(edge_tiles, adj))


def edge_kernel(block, pieces, late, hubs, counts, *refs):
    map_ref, hub_live_ref, tiles_ref, adj_ref, acc_ref = refs[:5]
    array_refs = refs[5 : 5 + counts]
    out_ref, late_ref, rhs_ref = refs[5 + counts :]
    me, loop = lax.axis_index("row"), lax.axis_index("loop")
    core = lax.rem(me, 2)
    size = tiles_ref.shape[1]
    rows, depth = adj_ref.shape
    cols = map_ref.shape[0] // (rows // size)
    slots = late_ref.shape[1] // len(late)
    per = slots // size
    for array, even, odd in hubs:
        shard = array_refs[array].shape[0]
        owner = loop ^ jnp.where(core == 0, even, odd)
        rhs_ref[pl.ds(pl.multiple_of(owner * shard, shard), shard), :] = array_refs[array][...]
    for n, (array, first, offset) in enumerate(pieces):
        rhs_ref[depth + n * slots : depth + (n + 1) * slots, :] = array_refs[array][first : first + slots, :]

    def body(m, _):
        blocks = []
        for i in range(block):
            row = m * block + i
            start = pl.multiple_of(row * size, size)
            line = []
            for b in range(depth // size):
                cell = adj_ref[pl.ds(start, size), b * size : (b + 1) * size]
                line.append(jnp.where(hub_live_ref[b, row] > 0, cell, jnp.zeros_like(cell)))
            for array, first, offset in pieces:
                for j in range(per):
                    line.append(cell_tile(tiles_ref, map_ref, row * cols + (me ^ offset) * per + j))
            blocks.append(jnp.concatenate(line, axis=1))
            for n, offset in enumerate(late):
                for j in range(per):
                    at = n * slots + j * size
                    late_ref[pl.ds(start, size), at : at + size] = cell_tile(
                        tiles_ref, map_ref, row * cols + (me ^ offset) * per + j
                    )
        span = pl.ds(pl.multiple_of(m * block * size, block * size), block * size)
        out_ref[span, :] = acc_ref[span, :] + dot(jnp.concatenate(blocks, axis=0), rhs_ref[...])
        return 0

    lax.fori_loop(0, rows // (block * size), body, 0)


def edge_term(pieces, late, hubs, slots, edge_map, hub_live, tiles, adj, acc, arrays):
    rows, depth = adj.shape
    deep = depth + len(pieces) * slots
    return pl.pallas_call(
        functools.partial(edge_kernel, 4, pieces, late, hubs, len(arrays)),
        out_shape=[jax.ShapeDtypeStruct(acc.shape, F32), jax.ShapeDtypeStruct((rows, len(late) * slots), BF)],
        in_specs=[SMEM, SMEM, VMEM, VMEM, VMEM] + [VMEM] * len(arrays),
        out_specs=[VMEM, VMEM],
        scratch_shapes=[pltpu.VMEM((deep, acc.shape[1]), BF)],
        compiler_params=params(16),
        cost_estimate=pl.CostEstimate(flops=0, bytes_accessed=0, transcendentals=0),
        name="edge",
    )(edge_map, hub_live, tiles, adj, acc, *arrays)


def last_kernel(block, counts, acc_ref, late_ref, weight_ref, *refs):
    array_refs = refs[:counts]
    out_ref, stage_ref, sems = refs[counts:]
    depth = array_refs[0].shape[0]
    for m in range(acc_ref.shape[0] // block):
        span = slice(m * block, (m + 1) * block)
        total = acc_ref[span, :]
        for n in range(counts):
            total += dot(late_ref[span, n * depth : (n + 1) * depth], array_refs[n][...])
        stage_ref[span, :] = jnp.maximum(dot(total.astype(BF), weight_ref[...]), 0.0).astype(BF)
        pltpu.make_async_copy(stage_ref.at[span], out_ref.at[span], sems.at[m]).start()
    for m in range(acc_ref.shape[0] // block):
        span = slice(m * block, (m + 1) * block)
        pltpu.make_async_copy(stage_ref.at[span], out_ref.at[span], sems.at[m]).wait()


def last_term(acc, late, weight, arrays):
    block = 512
    return pl.pallas_call(
        functools.partial(last_kernel, block, len(arrays)),
        out_shape=jax.ShapeDtypeStruct(acc.shape, BF),
        in_specs=[VMEM] * (3 + len(arrays)),
        out_specs=HBM,
        scratch_shapes=[pltpu.VMEM(acc.shape, BF), pltpu.SemaphoreType.DMA((acc.shape[0] // block,))],
        compiler_params=params(16),
        cost_estimate=pl.CostEstimate(flops=0, bytes_accessed=0, transcendentals=0),
        name="last",
    )(acc, late, weight, *arrays)


def swap(x, axis, offset):
    return lax.ppermute(x, axis, [(i, i ^ offset) for i in range(lax.axis_size(axis))])


def swap_by_core(x, even, odd):
    peers, ring = lax.axis_size("row"), lax.axis_size("loop")
    pairs = [(r * ring + l, r * ring + (l ^ (odd if r % 2 else even))) for r in range(peers) for l in range(ring)]
    return lax.ppermute(x, ("row", "loop"), pairs)


def per_device(
    features,
    weight,
    local_tiles,
    local_ids,
    local_live,
    send_rows,
    send_count,
    edge_tiles,
    edge_ids,
    edge_live,
    hub_feats,
    hub_adj,
    hub_live,
):
    peers, ring = lax.axis_size("row"), lax.axis_size("loop")
    slots = send_rows.shape[2]
    size = local_tiles.shape[1]
    tile_rows = features.shape[0] // size
    chips = range(2, peers, 2)
    early = [c for c in chips if c & (c - 1) == 0]
    late = [c ^ bit for c in chips if c & (c - 1) != 0 for bit in (0, 1)]
    offsets = [(c, c ^ 1) for c in early] + [(c,) for c in late] + [(1,), (0,)]
    feat, hub, tiles, local_map, edge_map, live, *packed = pack(
        offsets,
        send_rows[0],
        send_count,
        features,
        hub_feats,
        local_tiles,
        (local_ids, local_live, edge_ids, edge_live, hub_live.T),
        (tile_rows * tile_rows, tile_rows * (peers * slots // size)),
    )
    from_early = [swap(x, "row", c) for x, c in zip(packed, early)]
    from_late = [swap(x, "row", c) for x, c in zip(packed[len(early) :], late)]
    from_core, own = swap(packed[-2], "row", 1), packed[-1]
    arrays = [hub, swap(hub, "loop", 1)]
    hubs = [(0, 0, 0), (1, 1, 1)]
    halves = [swap_by_core(hub, offset, offset + 1) for offset in range(2, ring, 2)]
    acc, edges, adj = local_term(local_map, tiles, feat, edge_tiles, hub_adj)
    acc, *from_early = lax.optimization_barrier((acc, *from_early))
    shared = [swap(x, "row", 1) for x in from_early]
    acc, *halves = lax.optimization_barrier((acc, *halves))
    for n, got in enumerate(halves):
        hubs += [(len(arrays), 2 * n + 2, 2 * n + 3), (len(arrays) + 1, 2 * n + 3, 2 * n + 2)]
        arrays += [got, swap(got, "row", 1)]
    pieces = [(len(arrays), 0, 0), (len(arrays) + 1, 0, 1)]
    arrays += [own, from_core]
    for c, x, y in zip(early, from_early, shared):
        pieces += [(len(arrays), 0, c), (len(arrays) + 1, slots, c ^ 1)]
        arrays += [x, y]
    acc, late_tiles = edge_term(pieces, late, hubs, slots, edge_map, live, edges, adj, acc, arrays)
    return last_term(acc, late_tiles, weight, from_late)


def solution(mesh):
    both = ("row", "loop")
    placed = (
        P(both, None),
        P(),
        P(both, None, None),
        P(both),
        P(both),
        P(both, None, None),
        P(both, None),
        P(both, None, None),
        P(both),
        P(both),
        P("loop", None),
        P(both, None),
        P(both, None),
    )
    return jax.shard_map(per_device, mesh=mesh, in_specs=placed, out_specs=P(both, None), check_vma=False)
```

```python
import functools

import jax
import jax.numpy as jnp
from jax import lax
from jax.experimental import pallas as pl
from jax.experimental.pallas import tpu as pltpu
from jax.sharding import PartitionSpec as P

BF = jnp.bfloat16
F32 = jnp.float32
I32 = jnp.int32
VMEM = pl.BlockSpec(memory_space=pltpu.VMEM)
SMEM = pl.BlockSpec(memory_space=pltpu.SMEM)
HBM = pl.BlockSpec(memory_space=pltpu.HBM)
ANY = pl.BlockSpec(memory_space=pl.ANY)
MIB = 1 << 20
FREE = pl.CostEstimate(flops=0, bytes_accessed=0, transcendentals=0)
LONG = pl.CostEstimate(flops=1 << 35, bytes_accessed=0, transcendentals=0)


def params(mib):
    return pltpu.CompilerParams(vmem_limit_bytes=mib * MIB)


def hbm(*arrays):
    return [pltpu.with_memory_space_constraint(x, pltpu.HBM) for x in arrays]


def dot(a, b):
    return jnp.dot(a, b, preferred_element_type=F32)


def picks(send_ref, count_ref, rows, peer):
    slots = send_ref.shape[1]
    index = send_ref[pl.ds(peer, 1), :]
    slot = lax.broadcasted_iota(I32, (1, slots), 1)
    peers = lax.broadcasted_iota(I32, count_ref.shape, 1)
    count = jnp.sum(jnp.where(peers == peer, count_ref[...], 0), axis=1, keepdims=True)
    index = jnp.where(slot < count, index, -1)
    lane = lax.broadcasted_iota(I32, (128, 128), 1)
    blocks = []
    for part in range(slots // 128):
        column = jnp.broadcast_to(index[:, part * 128 : (part + 1) * 128], (128, 128)).T
        line = [jnp.where(column == lane + c * 128, 1.0, 0.0).astype(BF) for c in range(rows // 128)]
        blocks.append(jnp.concatenate(line, axis=1))
    return jnp.concatenate(blocks, axis=0)


def gather_groups(offsets, send_ref, count_ref, feat_ref, packed):
    me = lax.axis_index("row")
    rows = feat_ref.shape[0]
    for out_ref, group in zip(packed, offsets):
        hot = [picks(send_ref, count_ref, rows, me ^ offset) for offset in group]
        out_ref[...] = dot(jnp.concatenate(hot, axis=0), feat_ref[...]).astype(BF)


def start_all(sources, targets, sems):
    copies = [pltpu.make_async_copy(x, y, sems.at[n]) for n, (x, y) in enumerate(zip(sources, targets))]
    for copy in copies:
        copy.start()
    return copies


def wait_all(copies):
    for copy in copies:
        copy.wait()


def pack_kernel(offsets, feat_hbm, send_hbm, count_hbm, hub_hbm, tiles_hbm, *refs):
    sources = [feat_hbm, send_hbm, count_hbm, hub_hbm, tiles_hbm]
    targets, (*packed, sems) = refs[:5], refs[5:]
    copies = [pltpu.make_async_copy(x, y, sems.at[n]) for n, (x, y) in enumerate(zip(sources, targets))]
    for copy in copies[:4]:
        copy.start()
    wait_all(copies[:4])
    copies[4].start()
    feat_ref, send_ref, count_ref = targets[:3]
    gather_groups(offsets, send_ref, count_ref, feat_ref, packed)
    copies[4].wait()


def pack(offsets, features, send_rows, send_count, hub_feats, tiles):
    slots, width = send_rows.shape[1], features.shape[1]
    arrays = (features, send_rows, send_count, hub_feats, tiles)
    return pl.pallas_call(
        functools.partial(pack_kernel, offsets),
        out_shape=[jax.ShapeDtypeStruct(x.shape, x.dtype) for x in arrays]
        + [jax.ShapeDtypeStruct((len(group) * slots, width), BF) for group in offsets],
        in_specs=[HBM] * 5,
        out_specs=[VMEM] * (5 + len(offsets)),
        scratch_shapes=[pltpu.SemaphoreType.DMA((5,))],
        compiler_params=params(16),
        cost_estimate=FREE,
        name="pack",
    )(*hbm(*arrays))


def more_kernel(offsets, feat_ref, send_ref, count_ref, *packed):
    gather_groups(offsets, send_ref, count_ref, feat_ref, packed)


def pack_more(offsets, features, send_rows, send_count):
    slots, width = send_rows.shape[1], features.shape[1]
    return pl.pallas_call(
        functools.partial(more_kernel, offsets),
        out_shape=[jax.ShapeDtypeStruct((len(group) * slots, width), BF) for group in offsets],
        in_specs=[VMEM] * 3,
        out_specs=[VMEM] * len(offsets),
        compiler_params=params(16),
        cost_estimate=FREE,
        name="more",
    )(features, send_rows, send_count)


def fill_map(ids_ref, live_ref, map_ref):
    for cell in range(map_ref.shape[0]):
        map_ref[cell] = -1
    for t in range(ids_ref.shape[0]):
        map_ref[ids_ref[t]] = jnp.where(live_ref[t] > 0, t, -1)


def cell_tile(tiles_ref, map_ref, cell):
    slot = map_ref[cell]
    tile = tiles_ref[jnp.maximum(slot, 0)]
    return jnp.where(slot >= 0, tile, jnp.zeros_like(tile))


def edge_line(tiles_ref, map_ref, row, cols, sources, per):
    return [cell_tile(tiles_ref, map_ref, row * cols + source * per + j) for source in sources for j in range(per)]


def local_kernel(block, offsets, tiles_ref, feat_ref, send_ref, count_ref, near_ref, *refs):
    del near_ref
    sources, (out_ref, edge_ref, adj_ref, map_hbm, *refs) = refs[:6], refs[6:]
    packed = refs[: len(offsets)]
    *tables, local_map, edge_map, sems = refs[len(offsets) :]
    copies = start_all(sources, [*tables, edge_ref, adj_ref], sems)
    gather_groups(offsets, send_ref, count_ref, feat_ref, packed)
    wait_all(copies[:4])
    fill_map(tables[0], tables[1], local_map)
    fill_map(tables[2], tables[3], edge_map)
    copies.append(pltpu.make_async_copy(edge_map, map_hbm, sems.at[6]))
    copies[6].start()
    size = tiles_ref.shape[1]
    rows = feat_ref.shape[0]
    cols = rows // size

    def body(m, _):
        blocks = []
        for i in range(block):
            row = m * block + i
            line = [cell_tile(tiles_ref, local_map, row * cols + j) for j in range(cols)]
            blocks.append(jnp.concatenate(line, axis=1))
        span = pl.ds(pl.multiple_of(m * block * size, block * size), block * size)
        out_ref[span, :] = dot(jnp.concatenate(blocks, axis=0), feat_ref[...])
        return 0

    lax.fori_loop(0, rows // (block * size), body, 0)
    wait_all(copies[4:])


def local_term(offsets, tiles, features, send_rows, send_count, near, tables, edges, adj):
    rows, width = features.shape
    peers, slots = send_rows.shape
    size = tiles.shape[1]
    local_cells, edge_cells = (rows // size) ** 2, (rows // size) * (peers * slots // size)
    return pl.pallas_call(
        functools.partial(local_kernel, 8, offsets),
        out_shape=[jax.ShapeDtypeStruct(features.shape, F32)]
        + [jax.ShapeDtypeStruct(x.shape, BF) for x in (edges, adj)]
        + [jax.ShapeDtypeStruct((edge_cells,), I32)]
        + [jax.ShapeDtypeStruct((len(group) * slots, width), BF) for group in offsets],
        in_specs=[VMEM] * 5 + [HBM] * 6,
        out_specs=[VMEM] * 3 + [ANY] + [VMEM] * len(offsets),
        scratch_shapes=[pltpu.SMEM(x.shape, I32) for x in tables]
        + [pltpu.SMEM((local_cells,), I32), pltpu.SMEM((edge_cells,), I32), pltpu.SemaphoreType.DMA((7,))],
        compiler_params=params(16),
        cost_estimate=FREE,
        name="local",
    )(tiles, features, send_rows, send_count, near, *hbm(*tables, edges, adj))


def stack_kernel(*refs):
    out_ref, at = refs[-1], 0
    for ref in refs[:-1]:
        out_ref[at : at + ref.shape[0], :] = ref[...]
        at += ref.shape[0]


def stack(arrays):
    return pl.pallas_call(
        stack_kernel,
        out_shape=jax.ShapeDtypeStruct((sum(x.shape[0] for x in arrays), arrays[0].shape[1]), BF),
        in_specs=[VMEM] * len(arrays),
        out_specs=VMEM,
        compiler_params=params(16),
        cost_estimate=LONG,
        name="stack",
    )(*arrays)


def last_kernel(block, pieces, hubs, counts, *refs):
    map_hbm, live_hbm, edge_ref, adj_ref, acc_ref, weight_ref = refs[:6]
    array_refs = refs[6 : 6 + counts]
    out_ref, edge_map, live_ref, rhs_ref, stage_ref, sems = refs[6 + counts :]
    size = edge_ref.shape[1]
    rows, depth = adj_ref.shape
    steps = rows // (block * size)
    tables = [
        pltpu.make_async_copy(map_hbm, edge_map, sems.at[steps]),
        pltpu.make_async_copy(live_hbm, live_ref, sems.at[steps + 1]),
    ]
    for copy in tables:
        copy.start()
    me, loop = lax.axis_index("row"), lax.axis_index("loop")
    core = lax.rem(me, 2)
    slots = (rhs_ref.shape[0] - depth) // len(pieces)
    cols = edge_map.shape[0] // (rows // size)
    for array, even, odd in hubs:
        shard = array_refs[array].shape[0]
        owner = loop ^ jnp.where(core == 0, even, odd)
        rhs_ref[pl.ds(pl.multiple_of(owner * shard, shard), shard), :] = array_refs[array][...]
    for n, (array, first, _) in enumerate(pieces):
        rhs_ref[depth + n * slots : depth + (n + 1) * slots, :] = array_refs[array][first : first + slots, :]
    sources = [me ^ offset for _, _, offset in pieces]
    wait_all(tables)

    def write(m):
        span = pl.ds(pl.multiple_of(m * block * size, block * size), block * size)
        return pltpu.make_async_copy(stage_ref.at[span], out_ref.at[span], sems.at[m])

    def body(m, _):
        blocks = []
        for i in range(block):
            row = m * block + i
            start = pl.multiple_of(row * size, size)
            line = []
            for b in range(depth // size):
                cell = adj_ref[pl.ds(start, size), b * size : (b + 1) * size]
                line.append(jnp.where(live_ref[b, row] > 0, cell, jnp.zeros_like(cell)))
            line += edge_line(edge_ref, edge_map, row, cols, sources, slots // size)
            blocks.append(jnp.concatenate(line, axis=1))
        span = pl.ds(pl.multiple_of(m * block * size, block * size), block * size)
        total = (acc_ref[span, :] + dot(jnp.concatenate(blocks, axis=0), rhs_ref[...])).astype(BF)
        stage_ref[span, :] = jnp.maximum(dot(total, weight_ref[...]), 0.0).astype(BF)
        write(m).start()
        return 0

    lax.fori_loop(0, steps, body, 0)
    for m in range(steps):
        write(m).wait()


def last_term(pieces, hubs, slots, edge_map, hub_live, edges, adj, acc, weight, arrays):
    block = 8
    rows, width = acc.shape
    return pl.pallas_call(
        functools.partial(last_kernel, block, pieces, hubs, len(arrays)),
        out_shape=jax.ShapeDtypeStruct(acc.shape, BF),
        in_specs=[ANY, HBM] + [VMEM] * (4 + len(arrays)),
        out_specs=HBM,
        scratch_shapes=[
            pltpu.SMEM(edge_map.shape, I32),
            pltpu.SMEM(hub_live.shape, I32),
            pltpu.VMEM((adj.shape[1] + len(pieces) * slots, width), BF),
            pltpu.VMEM(acc.shape, BF),
            pltpu.SemaphoreType.DMA((rows // (block * edges.shape[1]) + 2,)),
        ],
        compiler_params=params(16),
        cost_estimate=FREE,
        name="last",
    )(edge_map, *hbm(hub_live), edges, adj, acc, weight, *arrays)


def swap(x, axis, offset):
    return lax.ppermute(x, axis, [(i, i ^ offset) for i in range(lax.axis_size(axis))])


def swap_by_core(x, even, odd):
    peers, ring = lax.axis_size("row"), lax.axis_size("loop")
    pairs = [(r * ring + l, r * ring + (l ^ (odd if r % 2 else even))) for r in range(peers) for l in range(ring)]
    return lax.ppermute(x, ("row", "loop"), pairs)


def per_device(
    features,
    weight,
    local_tiles,
    local_ids,
    local_live,
    send_rows,
    send_count,
    edge_tiles,
    edge_ids,
    edge_live,
    hub_feats,
    hub_adj,
    hub_live,
):
    peers, ring = lax.axis_size("row"), lax.axis_size("loop")
    slots = send_rows.shape[2]
    size = local_tiles.shape[1]
    tile_rows = features.shape[0] // size
    chips = range(2, peers, 2)
    early = [c for c in chips if c & (c - 1) == 0]
    late = [c ^ bit for c in chips if c not in early for bit in (0, 1)]
    feat, sends, counts, hub, tiles, *packed = pack(
        [(c, c ^ 1) for c in early], features, send_rows[0], send_count, hub_feats, local_tiles
    )
    from_early = [swap(x, "row", c) for x, c in zip(packed, early)]
    packed = pack_more([(c,) for c in late], feat, sends, counts)
    from_late = [swap(x, "row", c) for x, c in zip(packed, late)]
    near = swap(hub, "loop", 1)
    far = [swap_by_core(hub, offset, offset + 1) for offset in range(2, ring, 2)]
    acc, edges, adj, edge_map, to_core, own = local_term(
        [(1,), (0,)],
        tiles,
        feat,
        sends,
        counts,
        near,
        (local_ids, local_live, edge_ids, edge_live),
        edge_tiles,
        hub_adj,
    )
    from_core = swap(to_core, "row", 1)
    from_early = lax.optimization_barrier(tuple(from_early))
    acc, *ready = lax.optimization_barrier((acc, *from_early, *far))
    from_early, far = ready[: len(early)], ready[len(early) :]
    pieces, arrays = [(0, 0, 0), (1, 0, 1)], [own, from_core]
    for c, x in zip(early, from_early):
        pieces += [(len(arrays), 0, c), (len(arrays) + 1, slots, c ^ 1)]
        arrays += [x, swap(x, "row", 1)]
    pieces += [(len(arrays), n * slots, c) for n, c in enumerate(late)]
    arrays.append(stack(from_late))
    hubs = [(len(arrays), 0, 0), (len(arrays) + 1, 1, 1)]
    arrays += [hub, near]
    for n, x in enumerate(far):
        hubs += [(len(arrays), 2 * n + 2, 2 * n + 3), (len(arrays) + 1, 2 * n + 3, 2 * n + 2)]
        arrays += [x, swap(x, "row", 1)]
    return last_term(pieces, hubs, slots, edge_map, hub_live.T, edges, adj, acc, weight, arrays)


def solution(mesh):
    both = ("row", "loop")
    placed = (
        P(both, None),
        P(),
        P(both, None, None),
        P(both),
        P(both),
        P(both, None, None),
        P(both, None),
        P(both, None, None),
        P(both),
        P(both),
        P("loop", None),
        P(both, None),
        P(both, None),
    )
    return jax.shard_map(per_device, mesh=mesh, in_specs=placed, out_specs=P(both, None), check_vma=False)
```

```python
import functools

import jax
import jax.numpy as jnp
from jax import lax
from jax.experimental import pallas as pl
from jax.experimental.pallas import tpu as pltpu
from jax.sharding import PartitionSpec as P

BF = jnp.bfloat16
F32 = jnp.float32
I32 = jnp.int32
VMEM = pl.BlockSpec(memory_space=pltpu.VMEM)
SMEM = pl.BlockSpec(memory_space=pltpu.SMEM)
HBM = pl.BlockSpec(memory_space=pltpu.HBM)
ANY = pl.BlockSpec(memory_space=pl.ANY)
MIB = 1 << 20
FREE = pl.CostEstimate(flops=0, bytes_accessed=0, transcendentals=0)
VMEM = pl.BlockSpec(memory_space=pltpu.VMEM)
SMEM = pl.BlockSpec(memory_space=pltpu.SMEM)
HBM = pl.BlockSpec(memory_space=pltpu.HBM)
ANY = pl.BlockSpec(memory_space=pl.ANY)
MIB = 1 << 20
FREE = pl.CostEstimate(flops=0, bytes_accessed=0, transcendentals=0)
LONG = pl.CostEstimate(flops=1 << 35, bytes_accessed=0, transcendentals=0)


def params(mib):
    return pltpu.CompilerParams(vmem_limit_bytes=mib * MIB)


def hbm(*arrays):
    return [pltpu.with_memory_space_constraint(x, pltpu.HBM) for x in arrays]


def dot(a, b):
    return jnp.dot(a, b, preferred_element_type=F32)


def picks(send_ref, count_ref, rows, peer, scalar):
    slots = send_ref.shape[1]
    index = send_ref[pl.ds(peer, 1), :]
    slot = lax.broadcasted_iota(I32, (1, slots), 1)
    if scalar:
        count = count_ref[0, peer]
    else:
        peers = lax.broadcasted_iota(I32, count_ref.shape, 1)
        count = jnp.sum(jnp.where(peers == peer, count_ref[...], 0), axis=1, keepdims=True)
    index = jnp.where(slot < count, index, -1)
    lane = lax.broadcasted_iota(I32, (128, 128), 1)
    blocks = []
    for part in range(slots // 128):
        column = jnp.broadcast_to(index[:, part * 128 : (part + 1) * 128], (128, 128)).T
        line = [jnp.where(column == lane + c * 128, 1.0, 0.0).astype(BF) for c in range(rows // 128)]
        blocks.append(jnp.concatenate(line, axis=1))
    return jnp.concatenate(blocks, axis=0)


def gather_groups(offsets, send_ref, count_ref, feat_ref, packed, scalar=False):
    me = lax.axis_index("row")
    rows = feat_ref.shape[0]
    for out_ref, group in zip(packed, offsets):
        hot = [picks(send_ref, count_ref, rows, me ^ offset, scalar) for offset in group]
        out_ref[...] = dot(jnp.concatenate(hot, axis=0), feat_ref[...]).astype(BF)


def start_all(sources, targets, sems):
    copies = [pltpu.make_async_copy(x, y, sems.at[n]) for n, (x, y) in enumerate(zip(sources, targets))]
    for copy in copies:
        copy.start()
    return copies


def wait_all(copies):
    for copy in copies:
        copy.wait()


def pack_kernel(offsets, feat_hbm, send_hbm, count_hbm, hub_hbm, live_hbm, tiles_hbm, *refs):
    targets, (tiles_ref, *packed, scalars, sems) = refs[:5], refs[5:]
    feat_ref, send_ref = targets[:2]
    sources = [feat_hbm, send_hbm, count_hbm, hub_hbm, live_hbm, count_hbm]
    wait_all(start_all(sources, [*targets, scalars], sems))
    half = pl.ds(0, tiles_ref.shape[0] // 2)
    copy = pltpu.make_async_copy(tiles_hbm.at[half], tiles_ref.at[half], sems.at[6])
    copy.start()
    gather_groups(offsets, send_ref, scalars, feat_ref, packed, scalar=True)
    copy.wait()


def pack(offsets, features, send_rows, send_count, hub_feats, hub_live, tiles):
    slots, width = send_rows.shape[1], features.shape[1]
    arrays = (features, send_rows, send_count, hub_feats, hub_live, tiles)
    return pl.pallas_call(
        functools.partial(pack_kernel, offsets),
        out_shape=[jax.ShapeDtypeStruct(x.shape, x.dtype) for x in arrays]
        + [jax.ShapeDtypeStruct((len(group) * slots, width), BF) for group in offsets],
        in_specs=[HBM] * 6,
        out_specs=[VMEM] * (6 + len(offsets)),
        scratch_shapes=[pltpu.SMEM(send_count.shape, I32), pltpu.SemaphoreType.DMA((7,))],
        compiler_params=params(16),
        cost_estimate=FREE,
        name="pack",
    )(*hbm(*arrays))


def more_kernel(offsets, feat_ref, send_ref, count_ref, *packed):
    gather_groups(offsets, send_ref, count_ref, feat_ref, packed)


def pack_more(offsets, features, send_rows, send_count):
    slots, width = send_rows.shape[1], features.shape[1]
    return pl.pallas_call(
        functools.partial(more_kernel, offsets),
        out_shape=[jax.ShapeDtypeStruct((len(group) * slots, width), BF) for group in offsets],
        in_specs=[VMEM] * 3,
        out_specs=[VMEM] * len(offsets),
        compiler_params=params(16),
        cost_estimate=FREE,
        name="more",
    )(features, send_rows, send_count)


def fill_map(ids_ref, live_ref, map_ref):
    for cell in range(map_ref.shape[0]):
        map_ref[cell] = -1
    for t in range(ids_ref.shape[0]):
        map_ref[ids_ref[t]] = jnp.where(live_ref[t] > 0, t, -1)


def cell_tile(tiles_ref, map_ref, cell):
    slot = map_ref[cell]
    tile = tiles_ref[jnp.maximum(slot, 0)]
    return jnp.where(slot >= 0, tile, jnp.zeros_like(tile))


def edge_line(tiles_ref, map_ref, row, cols, sources, per):
    return [cell_tile(tiles_ref, map_ref, row * cols + source * per + j) for source in sources for j in range(per)]


def hub_line(adj_ref, live_ref, row, size, owners, per):
    line = []
    for owner in owners:
        for j in range(per):
            b = owner * per + j
            cell = adj_ref[pl.ds(pl.multiple_of(row * size, size), size), pl.ds(pl.multiple_of(b * size, size), size)]
            line.append(jnp.where(live_ref[b, row] > 0, cell, jnp.zeros_like(cell)))
    return line


def local_kernel(block, feat_ref, send_ref, count_ref, hub_ref, live_vmem, begun_ref, *refs):
    del begun_ref
    sources, (out_ref, tiles_ref, edge_ref, adj_ref, map_hbm, core_ref, *refs) = list(refs[:7]), refs[7:]
    *tables, local_map, edge_map, live_ref, own_ref, rhs_ref, sems = refs
    half = pl.ds(tiles_ref.shape[0] // 2, tiles_ref.shape[0] // 2)
    sources[4] = sources[4].at[half]
    copies = start_all([*sources, live_vmem], [*tables, tiles_ref.at[half], edge_ref, adj_ref, live_ref], sems)
    gather_groups([(1,), (0,)], send_ref, count_ref, feat_ref, [core_ref, own_ref])
    wait_all(copies[:4])
    fill_map(tables[0], tables[1], local_map)
    fill_map(tables[2], tables[3], edge_map)
    copies.append(pltpu.make_async_copy(edge_map, map_hbm, sems.at[8]))
    copies[8].start()
    copies[4].wait()
    size = tiles_ref.shape[1]
    rows = feat_ref.shape[0]
    cols, edge_cols = rows // size, edge_map.shape[0] // (rows // size)
    steps = rows // (block * size)

    def span(m):
        return pl.ds(pl.multiple_of(m * block * size, block * size), block * size)

    def local_body(m, _):
        blocks = []
        for i in range(block):
            row = m * block + i
            line = [cell_tile(tiles_ref, local_map, row * cols + j) for j in range(cols)]
            blocks.append(jnp.concatenate(line, axis=1))
        out_ref[span(m), :] = dot(jnp.concatenate(blocks, axis=0), feat_ref[...])
        return 0

    lax.fori_loop(0, steps, local_body, 0)
    wait_all(copies[5:])
    me, loop = lax.axis_index("row"), lax.axis_index("loop")
    shard, slots = hub_ref.shape[0], own_ref.shape[0]
    rhs_ref[:shard, :] = hub_ref[...]
    rhs_ref[shard:, :] = own_ref[...]

    def here_body(m, _):
        blocks = []
        for i in range(block):
            row = m * block + i
            line = hub_line(adj_ref, live_ref, row, size, [loop], shard // size)
            line += edge_line(edge_ref, edge_map, row, edge_cols, [me], slots // size)
            blocks.append(jnp.concatenate(line, axis=1))
        out_ref[span(m), :] += dot(jnp.concatenate(blocks, axis=0), rhs_ref[...])
        return 0

    lax.fori_loop(0, steps, here_body, 0)


def local_term(features, send_rows, send_count, hub, hub_live, begun, tables, tiles, edges, adj):
    rows, width = features.shape
    peers, slots = send_rows.shape
    size = tiles.shape[1]
    local_cells, edge_cells = (rows // size) ** 2, (rows // size) * (peers * slots // size)
    return pl.pallas_call(
        functools.partial(local_kernel, 8),
        out_shape=[
            jax.ShapeDtypeStruct(features.shape, F32),
            *[jax.ShapeDtypeStruct(x.shape, BF) for x in (tiles, edges, adj)],
            jax.ShapeDtypeStruct((edge_cells,), I32),
            jax.ShapeDtypeStruct((slots, width), BF),
        ],
        in_specs=[VMEM] * 6 + [HBM] * 7,
        out_specs=[VMEM] * 4 + [ANY, VMEM],
        scratch_shapes=[pltpu.SMEM(x.shape, I32) for x in tables]
        + [pltpu.SMEM((local_cells,), I32), pltpu.SMEM((edge_cells,), I32), pltpu.SMEM(hub_live.shape, I32)]
        + [pltpu.VMEM((slots, width), BF), pltpu.VMEM((hub.shape[0] + slots, width), BF)]
        + [pltpu.SemaphoreType.DMA((9,))],
        input_output_aliases={5: 1},
        compiler_params=params(16),
        cost_estimate=FREE,
        name="local",
    )(features, send_rows, send_count, hub, hub_live, begun, *hbm(*tables, tiles, edges, adj))


def sum_kernel(block, pieces, hubs, shard, counts, map_ref, live_vmem, edge_ref, adj_ref, acc_ref, *refs):
    array_refs, refs = refs[:counts], refs[counts:]
    last = len(refs) == 7
    if last:
        weight_ref, out_ref, edge_map, live_ref, rhs_ref, sems, stage_ref = refs
    else:
        out_ref, edge_map, live_ref, rhs_ref, sems = refs
    size = edge_ref.shape[1]
    rows = adj_ref.shape[0]
    steps = rows // (block * size)
    tables = [
        pltpu.make_async_copy(map_ref, edge_map, sems.at[steps]),
        pltpu.make_async_copy(live_vmem, live_ref, sems.at[steps + 1]),
    ]
    for copy in tables:
        copy.start()
    me, loop = lax.axis_index("row"), lax.axis_index("loop")
    core = lax.rem(me, 2)
    cols = edge_map.shape[0] // (rows // size)
    owners = [loop ^ jnp.where(core == 0, even, odd) for _, _, even, odd in hubs]
    sources = [me ^ offset for _, _, offset in pieces]
    at = 0
    for array, first, _, _ in hubs:
        rhs_ref[at : at + shard, :] = array_refs[array][first : first + shard, :]
        at += shard
    slots = (rhs_ref.shape[0] - at) // len(pieces)
    for array, first, _ in pieces:
        rhs_ref[at : at + slots, :] = array_refs[array][first : first + slots, :]
        at += slots
    wait_all(tables)

    def write(m):
        span = pl.ds(pl.multiple_of(m * block * size, block * size), block * size)
        return pltpu.make_async_copy(stage_ref.at[span], out_ref.at[span], sems.at[m])

    def body(m, _):
        blocks = []
        for i in range(block):
            row = m * block + i
            line = hub_line(adj_ref, live_ref, row, size, owners, shard // size)
            line += edge_line(edge_ref, edge_map, row, cols, sources, slots // size)
            blocks.append(jnp.concatenate(line, axis=1))
        span = pl.ds(pl.multiple_of(m * block * size, block * size), block * size)
        total = acc_ref[span, :] + dot(jnp.concatenate(blocks, axis=0), rhs_ref[...])
        if last:
            stage_ref[span, :] = jnp.maximum(dot(total.astype(BF), weight_ref[...]), 0.0).astype(BF)
            write(m).start()
        else:
            out_ref[span, :] = total
        return 0

    lax.fori_loop(0, steps, body, 0)
    if last:
        for m in range(steps):
            write(m).wait()


def sum_term(name, pieces, hubs, shard, slots, edge_map, hub_live, edges, adj, acc, arrays, weight=None):
    block = 8
    rows, width = acc.shape
    last = weight is not None
    deep = len(pieces) * slots + len(hubs) * shard
    return pl.pallas_call(
        functools.partial(sum_kernel, block, pieces, hubs, shard, len(arrays)),
        out_shape=jax.ShapeDtypeStruct(acc.shape, BF if last else F32),
        in_specs=[ANY] + [VMEM] * (4 + len(arrays) + last),
        out_specs=HBM if last else VMEM,
        scratch_shapes=[
            pltpu.SMEM(edge_map.shape, I32),
            pltpu.SMEM(hub_live.shape, I32),
            pltpu.VMEM((deep, width), BF),
            pltpu.SemaphoreType.DMA((rows // (block * edges.shape[1]) + 2,)),
        ]
        + [pltpu.VMEM(acc.shape, BF)] * last,
        compiler_params=params(16),
        cost_estimate=FREE,
        name=name,
    )(edge_map, hub_live, edges, adj, acc, *arrays, *([weight] if last else []))


def swap(x, axis, offset):
    return lax.ppermute(x, axis, [(i, i ^ offset) for i in range(lax.axis_size(axis))])


def swap_by_core(x, even, odd):
    peers, ring = lax.axis_size("row"), lax.axis_size("loop")
    pairs = [(r * ring + l, r * ring + (l ^ (odd if r % 2 else even))) for r in range(peers) for l in range(ring)]
    return lax.ppermute(x, ("row", "loop"), pairs)


def per_device(
    features,
    weight,
    local_tiles,
    local_ids,
    local_live,
    send_rows,
    send_count,
    edge_tiles,
    edge_ids,
    edge_live,
    hub_feats,
    hub_adj,
    hub_live,
):
    peers, ring = lax.axis_size("row"), lax.axis_size("loop")
    slots = send_rows.shape[2]
    size = local_tiles.shape[1]
    tile_rows = features.shape[0] // size
    chips = range(2, peers, 2)
    early = [c for c in chips if c & (c - 1) == 0]
    late = [c for c in chips if c not in early]
    feat, sends, counts, hub, live, tiles, *packed = pack(
        [(c, c ^ 1) for c in early], features, send_rows[0], send_count, hub_feats, hub_live.T, local_tiles
    )
    from_early = [swap(x, "row", c) for x, c in zip(packed, early)]
    packed = pack_more([(c, c ^ 1) for c in late], feat, sends, counts)
    from_late = [swap(x, "row", c) for x, c in zip(packed, late)]
    near = swap(hub, "loop", 1)
    far = [swap_by_core(hub, offset, offset + 1) for offset in range(2, ring, 2)]
    acc, _, edges, adj, edge_map, to_core = local_term(
        feat,
        sends,
        counts,
        hub,
        live,
        tiles,
        (local_ids, local_live, edge_ids, edge_live),
        local_tiles,
        edge_tiles,
        hub_adj,
    )
    from_core = swap(to_core, "row", 1)
    from_early = lax.optimization_barrier(tuple(from_early))
    acc, near, *ready = lax.optimization_barrier((acc, near, *from_early, *from_late, *far))
    arrived, far = ready[: len(chips)], ready[len(chips) :]
    shared = [swap(x, "row", 1) for x in arrived]
    far_shared = [swap(x, "row", 1) for x in far]
    common = (hub.shape[0], slots, edge_map, live, edges, adj)
    order = early + late
    pieces = [(n, 0, c) for n, c in enumerate(order)]
    acc = sum_term("middle", pieces, [(len(chips), 0, 1, 1)], *common, acc, [*arrived, near])
    arrays = [from_core, *shared, *far, *far_shared]
    pieces = [(0, 0, 1)] + [(1 + n, slots, c ^ 1) for n, c in enumerate(order)]
    at = len(pieces)
    hubs = [(at + n, 0, 2 * n + 2, 2 * n + 3) for n in range(len(far))]
    hubs += [(at + len(far) + n, 0, 2 * n + 3, 2 * n + 2) for n in range(len(far))]
    return sum_term("last", pieces, hubs, *common, acc, arrays, weight)


def solution(mesh):
    both = ("row", "loop")
    placed = (
        P(both, None),
        P(),
        P(both, None, None),
        P(both),
        P(both),
        P(both, None, None),
        P(both, None),
        P(both, None, None),
        P(both),
        P(both),
        P("loop", None),
        P(both, None),
        P(both, None),
    )
    return jax.shard_map(per_device, mesh=mesh, in_specs=placed, out_specs=P(both, None), check_vma=False)
```

```python
import functools

import jax
import jax.numpy as jnp
from jax import lax
from jax.experimental import pallas as pl
from jax.experimental.pallas import tpu as pltpu
from jax.sharding import PartitionSpec as P

BF = jnp.bfloat16
F32 = jnp.float32
I32 = jnp.int32
LONG = pl.CostEstimate(flops=1 << 35, bytes_accessed=0, transcendentals=0)
VMEM = pl.BlockSpec(memory_space=pltpu.VMEM)
SMEM = pl.BlockSpec(memory_space=pltpu.SMEM)
HBM = pl.BlockSpec(memory_space=pltpu.HBM)
ANY = pl.BlockSpec(memory_space=pl.ANY)
MIB = 1 << 20
FREE = pl.CostEstimate(flops=0, bytes_accessed=0, transcendentals=0)
VMEM = pl.BlockSpec(memory_space=pltpu.VMEM)
SMEM = pl.BlockSpec(memory_space=pltpu.SMEM)
HBM = pl.BlockSpec(memory_space=pltpu.HBM)
ANY = pl.BlockSpec(memory_space=pl.ANY)
MIB = 1 << 20
FREE = pl.CostEstimate(flops=0, bytes_accessed=0, transcendentals=0)
LONG = pl.CostEstimate(flops=1 << 35, bytes_accessed=0, transcendentals=0)


def params(mib):
    return pltpu.CompilerParams(vmem_limit_bytes=mib * MIB)


def hbm(*arrays):
    return [pltpu.with_memory_space_constraint(x, pltpu.HBM) for x in arrays]


def dot(a, b):
    return jnp.dot(a, b, preferred_element_type=F32)


def picks(send_ref, count_ref, rows, peer, scalar):
    slots = send_ref.shape[1]
    index = send_ref[pl.ds(peer, 1), :]
    slot = lax.broadcasted_iota(I32, (1, slots), 1)
    if scalar:
        count = count_ref[0, peer]
    else:
        peers = lax.broadcasted_iota(I32, count_ref.shape, 1)
        count = jnp.sum(jnp.where(peers == peer, count_ref[...], 0), axis=1, keepdims=True)
    index = jnp.where(slot < count, index, -1)
    lane = lax.broadcasted_iota(I32, (128, 128), 1)
    blocks = []
    for part in range(slots // 128):
        column = jnp.broadcast_to(index[:, part * 128 : (part + 1) * 128], (128, 128)).T
        line = [jnp.where(column == lane + c * 128, 1.0, 0.0).astype(BF) for c in range(rows // 128)]
        blocks.append(jnp.concatenate(line, axis=1))
    return jnp.concatenate(blocks, axis=0)


def gather_groups(offsets, send_ref, count_ref, feat_ref, packed, scalar=False):
    me = lax.axis_index("row")
    rows = feat_ref.shape[0]
    for out_ref, group in zip(packed, offsets):
        hot = [picks(send_ref, count_ref, rows, me ^ offset, scalar) for offset in group]
        out_ref[...] = dot(jnp.concatenate(hot, axis=0), feat_ref[...]).astype(BF)


def start_all(sources, targets, sems):
    copies = [pltpu.make_async_copy(x, y, sems.at[n]) for n, (x, y) in enumerate(zip(sources, targets))]
    for copy in copies:
        copy.start()
    return copies


def wait_all(copies):
    for copy in copies:
        copy.wait()


def pack_kernel(offsets, feat_hbm, send_hbm, count_hbm, hub_hbm, live_hbm, *refs):
    targets, (*packed, scalars, sems) = refs[:5], refs[5:]
    feat_ref, send_ref = targets[:2]
    sources = [feat_hbm, send_hbm, count_hbm, hub_hbm, live_hbm, count_hbm]
    copies = start_all(sources, [*targets, scalars], sems)
    wait_all(copies[:2] + copies[5:])
    gather_groups(offsets, send_ref, scalars, feat_ref, packed, scalar=True)
    wait_all(copies[2:5])


def pack(offsets, features, send_rows, send_count, hub_feats, hub_live):
    slots, width = send_rows.shape[1], features.shape[1]
    arrays = (features, send_rows, send_count, hub_feats, hub_live)
    return pl.pallas_call(
        functools.partial(pack_kernel, offsets),
        out_shape=[jax.ShapeDtypeStruct(x.shape, x.dtype) for x in arrays]
        + [jax.ShapeDtypeStruct((len(group) * slots, width), BF) for group in offsets],
        in_specs=[HBM] * 5,
        out_specs=[VMEM] * (5 + len(offsets)),
        scratch_shapes=[pltpu.SMEM(send_count.shape, I32), pltpu.SemaphoreType.DMA((6,))],
        compiler_params=params(16),
        cost_estimate=FREE,
        name="pack",
    )(*hbm(*arrays))


def more_kernel(offsets, feat_ref, send_ref, count_ref, tiles_hbm, tiles_ref, *refs):
    *packed, sem = refs
    half = pl.ds(0, tiles_ref.shape[0] // 2)
    copy = pltpu.make_async_copy(tiles_hbm.at[half], tiles_ref.at[half], sem)
    copy.start()
    gather_groups(offsets, send_ref, count_ref, feat_ref, packed)
    copy.wait()


def pack_more(offsets, features, send_rows, send_count, tiles):
    slots, width = send_rows.shape[1], features.shape[1]
    return pl.pallas_call(
        functools.partial(more_kernel, offsets),
        out_shape=[jax.ShapeDtypeStruct(tiles.shape, BF)]
        + [jax.ShapeDtypeStruct((len(group) * slots, width), BF) for group in offsets],
        in_specs=[VMEM] * 3 + [HBM],
        out_specs=[VMEM] * (1 + len(offsets)),
        scratch_shapes=[pltpu.SemaphoreType.DMA],
        compiler_params=params(16),
        cost_estimate=FREE,
        name="more",
    )(features, send_rows, send_count, *hbm(tiles))


def clear_map(map_ref):
    for cell in range(map_ref.shape[0]):
        map_ref[cell] = -1


def fill_map(ids_ref, live_ref, map_ref, first, count):
    for n in range(count):
        t = first + n
        map_ref[ids_ref[t]] = jnp.where(live_ref[t] > 0, t, -1)


def cell_tile(tiles_ref, map_ref, cell):
    slot = map_ref[cell]
    tile = tiles_ref[jnp.maximum(slot, 0)]
    return jnp.where(slot >= 0, tile, jnp.zeros_like(tile))


def edge_line(tiles_ref, map_ref, row, cols, sources, per):
    return [cell_tile(tiles_ref, map_ref, row * cols + source * per + j) for source in sources for j in range(per)]


def local_kernel(block, feat_ref, send_ref, count_ref, begun_ref, *refs):
    del begun_ref
    sources, (out_ref, tiles_ref, edge_ref, adj_ref, map_hbm, core_ref, *refs) = list(refs[:7]), refs[7:]
    *tables, local_map, edge_map, own_ref, sems = refs
    half = pl.ds(tiles_ref.shape[0] // 2, tiles_ref.shape[0] // 2)
    sources[4] = sources[4].at[half]
    copies = start_all(sources, [*tables, tiles_ref.at[half], edge_ref, adj_ref], sems)
    gather_groups([(1,)], send_ref, count_ref, feat_ref, [core_ref])
    wait_all(copies[:4])
    clear_map(local_map)
    fill_map(tables[0], tables[1], local_map, 0, tables[0].shape[0])
    clear_map(edge_map)
    gather_groups([(0,)], send_ref, count_ref, feat_ref, [own_ref])
    copies[4].wait()
    size = tiles_ref.shape[1]
    rows = feat_ref.shape[0]
    cols, edge_cols = rows // size, edge_map.shape[0] // (rows // size)
    steps = rows // (block * size)
    share = tables[2].shape[0] // steps

    def span(m):
        return pl.ds(pl.multiple_of(m * block * size, block * size), block * size)

    def local_body(m, _):
        blocks = []
        for i in range(block):
            row = m * block + i
            line = [cell_tile(tiles_ref, local_map, row * cols + j) for j in range(cols)]
            blocks.append(jnp.concatenate(line, axis=1))
        out_ref[span(m), :] = dot(jnp.concatenate(blocks, axis=0), feat_ref[...])
        fill_map(tables[2], tables[3], edge_map, m * share, share)
        return 0

    lax.fori_loop(0, steps, local_body, 0)
    fill_map(tables[2], tables[3], edge_map, steps * share, tables[2].shape[0] - steps * share)
    copies.append(pltpu.make_async_copy(edge_map, map_hbm, sems.at[7]))
    copies[7].start()
    copies[5].wait()
    me = lax.axis_index("row")
    per = own_ref.shape[0] // size

    def own_body(m, _):
        lines = [edge_line(edge_ref, edge_map, m * block + i, edge_cols, [me], per) for i in range(block)]
        own_tiles = jnp.concatenate([jnp.concatenate(line, axis=1) for line in lines], axis=0)
        out_ref[span(m), :] += dot(own_tiles, own_ref[...])
        return 0

    lax.fori_loop(0, steps, own_body, 0)
    wait_all(copies[6:])


def local_term(features, send_rows, send_count, begun, tables, tiles, edges, adj):
    rows, width = features.shape
    peers, slots = send_rows.shape
    size = tiles.shape[1]
    local_cells, edge_cells = (rows // size) ** 2, (rows // size) * (peers * slots // size)
    return pl.pallas_call(
        functools.partial(local_kernel, 8),
        out_shape=[
            jax.ShapeDtypeStruct(features.shape, F32),
            *[jax.ShapeDtypeStruct(x.shape, BF) for x in (tiles, edges, adj)],
            jax.ShapeDtypeStruct((edge_cells,), I32),
            jax.ShapeDtypeStruct((slots, width), BF),
        ],
        in_specs=[VMEM] * 4 + [HBM] * 7,
        out_specs=[VMEM] * 4 + [ANY, VMEM],
        scratch_shapes=[pltpu.SMEM(x.shape, I32) for x in tables]
        + [pltpu.SMEM((local_cells,), I32), pltpu.SMEM((edge_cells,), I32)]
        + [pltpu.VMEM((slots, width), BF), pltpu.SemaphoreType.DMA((8,))],
        input_output_aliases={3: 1},
        compiler_params=params(16),
        cost_estimate=FREE,
        name="local",
    )(features, send_rows, send_count, begun, *hbm(*tables, tiles, edges, adj))


def masked_line(adj_ref, mask_ref, row, size, columns):
    span = pl.ds(pl.multiple_of(row * size, size), size)
    line = []
    for column in columns:
        mask = jnp.broadcast_to(mask_ref[pl.ds(row, 1), column], (size, column.size)).astype(BF)
        line.append(adj_ref[span, column] * mask)
    return jnp.concatenate(line, axis=1)


def hub_kernel(block, hubs, waited, live_ref, adj_ref, acc_ref, *refs):
    *array_refs, out_ref, mask_ref, rhs_ref = refs[waited:]
    core, loop = lax.rem(lax.axis_index("row"), 2), lax.axis_index("loop")
    shard = array_refs[0].shape[0]
    tiles, rows = live_ref.shape
    size = adj_ref.shape[0] // rows
    columns = []
    for n, (array_ref, (even, odd)) in enumerate(zip(array_refs, hubs)):
        owner = loop ^ jnp.where(core == 0, even, odd)
        columns.append(pl.ds(pl.multiple_of(owner * shard, shard), shard))
        rhs_ref[n * shard : (n + 1) * shard, :] = array_ref[...]
    lane = lax.broadcasted_iota(I32, (tiles, adj_ref.shape[1]), 1)
    first = lax.broadcasted_iota(I32, (tiles, adj_ref.shape[1]), 0) * size
    inside = (lane >= first) & (lane < first + size)
    live = live_ref[...]
    for row in range(rows):
        hit = jnp.where(inside & (live[:, row : row + 1] > 0), 1.0, 0.0)
        mask_ref[row : row + 1, :] = jnp.sum(hit, axis=0, keepdims=True)

    def body(m, _):
        blocks = [masked_line(adj_ref, mask_ref, m * block + i, size, columns) for i in range(block)]
        span = pl.ds(pl.multiple_of(m * block * size, block * size), block * size)
        out_ref[span, :] = acc_ref[span, :] + dot(jnp.concatenate(blocks, axis=0), rhs_ref[...])
        return 0

    lax.fori_loop(0, rows // block, body, 0)


def hub_term(hubs, waited, hub_live, adj, acc, arrays):
    shard, width = arrays[0].shape
    return pl.pallas_call(
        functools.partial(hub_kernel, 8, hubs, len(waited)),
        out_shape=[
            jax.ShapeDtypeStruct(acc.shape, F32),
            jax.ShapeDtypeStruct((hub_live.shape[1], adj.shape[1]), F32),
        ],
        in_specs=[VMEM] * (3 + len(waited) + len(arrays)),
        out_specs=[VMEM] * 2,
        scratch_shapes=[pltpu.VMEM((len(hubs) * shard, width), BF)],
        compiler_params=params(16),
        cost_estimate=LONG,
        name="hub",
    )(hub_live, adj, acc, *waited, *arrays)


def last_kernel(block, pieces, map_ref, edge_ref, adj_ref, mask_ref, acc_ref, weight_ref, near_ref, *refs):
    *array_refs, out_ref, edge_map, rhs_ref, total_ref, stage_ref, sems = refs
    size = edge_ref.shape[1]
    rows = acc_ref.shape[0]
    steps = rows // (block * size)
    table = pltpu.make_async_copy(map_ref, edge_map, sems.at[steps])
    table.start()
    me, loop = lax.axis_index("row"), lax.axis_index("loop")
    cols = edge_map.shape[0] // (rows // size)
    slots = rhs_ref.shape[0] // len(pieces)
    shard = near_ref.shape[0]
    for n, (array, first, _) in enumerate(pieces):
        rhs_ref[n * slots : (n + 1) * slots, :] = array_refs[array][first : first + slots, :]
    sources = [me ^ offset for _, _, offset in pieces]
    columns = [pl.ds(pl.multiple_of((loop ^ 1) * shard, shard), shard)]

    def span(m):
        return pl.ds(pl.multiple_of(m * block * size, block * size), block * size)

    def write(m):
        return pltpu.make_async_copy(stage_ref.at[span(m)], out_ref.at[span(m)], sems.at[m])

    def near_body(m, _):
        blocks = [masked_line(adj_ref, mask_ref, m * block + i, size, columns) for i in range(block)]
        total_ref[span(m), :] = acc_ref[span(m), :] + dot(jnp.concatenate(blocks, axis=0), near_ref[...])
        return 0

    lax.fori_loop(0, steps, near_body, 0)
    table.wait()

    def body(m, _):
        lines = [
            edge_line(edge_ref, edge_map, m * block + i, cols, sources, slots // size) for i in range(block)
        ]
        tiles = jnp.concatenate([jnp.concatenate(line, axis=1) for line in lines], axis=0)
        total = total_ref[span(m), :] + dot(tiles, rhs_ref[...])
        stage_ref[span(m), :] = jnp.maximum(dot(total.astype(BF), weight_ref[...]), 0.0).astype(BF)
        write(m).start()
        return 0

    lax.fori_loop(0, steps, body, 0)
    for m in range(steps):
        write(m).wait()


def last_term(pieces, slots, edge_map, edges, adj, mask, acc, weight, near, arrays):
    block = 8
    rows, width = acc.shape
    return pl.pallas_call(
        functools.partial(last_kernel, block, pieces),
        out_shape=jax.ShapeDtypeStruct(acc.shape, BF),
        in_specs=[ANY] + [VMEM] * (6 + len(arrays)),
        out_specs=HBM,
        scratch_shapes=[
            pltpu.SMEM(edge_map.shape, I32),
            pltpu.VMEM((len(pieces) * slots, width), BF),
            pltpu.VMEM(acc.shape, F32),
            pltpu.VMEM(acc.shape, BF),
            pltpu.SemaphoreType.DMA((rows // (block * edges.shape[1]) + 1,)),
        ],
        compiler_params=params(16),
        cost_estimate=FREE,
        name="last",
    )(edge_map, edges, adj, mask, acc, weight, near, *arrays)


def swap(x, axis, offset):
    return lax.ppermute(x, axis, [(i, i ^ offset) for i in range(lax.axis_size(axis))])


def swap_by_core(x, even, odd):
    peers, ring = lax.axis_size("row"), lax.axis_size("loop")
    pairs = [(r * ring + l, r * ring + (l ^ (odd if r % 2 else even))) for r in range(peers) for l in range(ring)]
    return lax.ppermute(x, ("row", "loop"), pairs)


def per_device(
    features,
    weight,
    local_tiles,
    local_ids,
    local_live,
    send_rows,
    send_count,
    edge_tiles,
    edge_ids,
    edge_live,
    hub_feats,
    hub_adj,
    hub_live,
):
    peers, ring = lax.axis_size("row"), lax.axis_size("loop")
    slots = send_rows.shape[2]
    size = local_tiles.shape[1]
    tile_rows = features.shape[0] // size
    chips = range(2, peers, 2)
    near_chips = [c for c in chips if c & (c - 1) == 0]
    far_chips = [c for c in chips if c not in near_chips]
    feat, sends, counts, hub, live, *packed = pack(
        [(c, c ^ 1) for c in far_chips], features, send_rows[0], send_count, hub_feats, hub_live.T
    )
    from_far = [swap(x, "row", c) for x, c in zip(packed, far_chips)]
    tiles, *packed = pack_more([(c, c ^ 1) for c in near_chips], feat, sends, counts, local_tiles)
    from_near = [swap(x, "row", c) for x, c in zip(packed, near_chips)]
    near = swap(hub, "loop", 1)
    far = [swap_by_core(hub, offset, offset + 1) for offset in range(2, ring, 2)]
    acc, _, edges, adj, edge_map, to_core = local_term(
        feat,
        sends,
        counts,
        tiles,
        (local_ids, local_live, edge_ids, edge_live),
        local_tiles,
        edge_tiles,
        hub_adj,
    )
    from_core = swap(to_core, "row", 1)
    acc, near, *far = lax.optimization_barrier((acc, near, *far))
    from_far = lax.optimization_barrier(tuple(from_far))
    acc, *arrived = lax.optimization_barrier((acc, *from_far, *from_near))
    shared = [swap(x, "row", 1) for x in arrived]
    far_shared = [swap(x, "row", 1) for x in far]
    hubs, arrays = [(0, 0)], [hub]
    for n, (x, y) in enumerate(zip(far, far_shared)):
        hubs += [(2 * n + 2, 2 * n + 3), (2 * n + 3, 2 * n + 2)]
        arrays += [x, y]
    acc, mask = hub_term(hubs, [from_core], live, adj, acc, arrays)
    pieces = [(0, 0, 1)]
    for n, c in enumerate(far_chips + near_chips):
        pieces += [(1 + n, 0, c), (1 + len(chips) + n, slots, c ^ 1)]
    return last_term(pieces, slots, edge_map, edges, adj, mask, acc, weight, near, [from_core, *arrived, *shared])


def solution(mesh):
    both = ("row", "loop")
    placed = (
        P(both, None),
        P(),
        P(both, None, None),
        P(both),
        P(both),
        P(both, None, None),
        P(both, None),
        P(both, None, None),
        P(both),
        P(both),
        P("loop", None),
        P(both, None),
        P(both, None),
    )
    return jax.shard_map(per_device, mesh=mesh, in_specs=placed, out_specs=P(both, None), check_vma=False)
```

```python
import functools

import jax
import jax.numpy as jnp
from jax import lax
from jax.experimental import pallas as pl
from jax.experimental.pallas import tpu as pltpu
from jax.sharding import PartitionSpec as P

BF = jnp.bfloat16
F32 = jnp.float32
I32 = jnp.int32
EARLY = pl.CostEstimate(flops=1 << 35, bytes_accessed=0, transcendentals=0)
VMEM = pl.BlockSpec(memory_space=pltpu.VMEM)
SMEM = pl.BlockSpec(memory_space=pltpu.SMEM)
HBM = pl.BlockSpec(memory_space=pltpu.HBM)
ANY = pl.BlockSpec(memory_space=pl.ANY)
MIB = 1 << 20
FREE = pl.CostEstimate(flops=0, bytes_accessed=0, transcendentals=0)
VMEM = pl.BlockSpec(memory_space=pltpu.VMEM)
SMEM = pl.BlockSpec(memory_space=pltpu.SMEM)
HBM = pl.BlockSpec(memory_space=pltpu.HBM)
ANY = pl.BlockSpec(memory_space=pl.ANY)
MIB = 1 << 20
FREE = pl.CostEstimate(flops=0, bytes_accessed=0, transcendentals=0)
EARLY = pl.CostEstimate(flops=1 << 35, bytes_accessed=0, transcendentals=0)
LONG = pl.CostEstimate(flops=1 << 35, bytes_accessed=0, transcendentals=0)


def params(mib):
    return pltpu.CompilerParams(vmem_limit_bytes=mib * MIB)


def hbm(*arrays):
    return [pltpu.with_memory_space_constraint(x, pltpu.HBM) for x in arrays]


def dot(a, b):
    return jnp.dot(a, b, preferred_element_type=F32)


def picks(send_ref, count_ref, rows, peer, scalar):
    slots = send_ref.shape[1]
    index = send_ref[pl.ds(peer, 1), :]
    slot = lax.broadcasted_iota(I32, (1, slots), 1)
    if scalar:
        count = count_ref[0, peer]
    else:
        peers = lax.broadcasted_iota(I32, count_ref.shape, 1)
        count = jnp.sum(jnp.where(peers == peer, count_ref[...], 0), axis=1, keepdims=True)
    index = jnp.where(slot < count, index, -1)
    lane = lax.broadcasted_iota(I32, (128, 128), 1)
    blocks = []
    for part in range(slots // 128):
        column = jnp.broadcast_to(index[:, part * 128 : (part + 1) * 128], (128, 128)).T
        line = [jnp.where(column == lane + c * 128, 1.0, 0.0).astype(BF) for c in range(rows // 128)]
        blocks.append(jnp.concatenate(line, axis=1))
    return jnp.concatenate(blocks, axis=0)


def gather_groups(offsets, send_ref, count_ref, feat_ref, packed, scalar=False):
    me = lax.axis_index("row")
    rows = feat_ref.shape[0]
    for out_ref, group in zip(packed, offsets):
        hot = [picks(send_ref, count_ref, rows, me ^ offset, scalar) for offset in group]
        out_ref[...] = dot(jnp.concatenate(hot, axis=0), feat_ref[...]).astype(BF)


def start_all(sources, targets, sems):
    copies = [pltpu.make_async_copy(x, y, sems.at[n]) for n, (x, y) in enumerate(zip(sources, targets))]
    for copy in copies:
        copy.start()
    return copies


def wait_all(copies):
    for copy in copies:
        copy.wait()


def pack_kernel(offsets, feat_hbm, send_hbm, count_hbm, hub_hbm, live_hbm, *refs):
    targets, (*packed, scalars, sems) = refs[:5], refs[5:]
    feat_ref, send_ref = targets[:2]
    sources = [feat_hbm, send_hbm, count_hbm, hub_hbm, live_hbm, count_hbm]
    copies = start_all(sources, [*targets, scalars], sems)
    wait_all(copies[:2] + copies[5:])
    gather_groups(offsets, send_ref, scalars, feat_ref, packed, scalar=True)
    wait_all(copies[2:5])


def pack(offsets, features, send_rows, send_count, hub_feats, hub_live):
    slots, width = send_rows.shape[1], features.shape[1]
    arrays = (features, send_rows, send_count, hub_feats, hub_live)
    return pl.pallas_call(
        functools.partial(pack_kernel, offsets),
        out_shape=[jax.ShapeDtypeStruct(x.shape, x.dtype) for x in arrays]
        + [jax.ShapeDtypeStruct((len(group) * slots, width), BF) for group in offsets],
        in_specs=[HBM] * 5,
        out_specs=[VMEM] * (5 + len(offsets)),
        scratch_shapes=[pltpu.SMEM(send_count.shape, I32), pltpu.SemaphoreType.DMA((6,))],
        compiler_params=params(16),
        cost_estimate=EARLY,
        name="pack",
    )(*hbm(*arrays))


def more_kernel(offsets, feat_ref, send_ref, count_ref, *packed):
    gather_groups(offsets, send_ref, count_ref, feat_ref, packed)


def pack_more(offsets, features, send_rows, send_count):
    slots, width = send_rows.shape[1], features.shape[1]
    return pl.pallas_call(
        functools.partial(more_kernel, offsets),
        out_shape=[jax.ShapeDtypeStruct((len(group) * slots, width), BF) for group in offsets],
        in_specs=[VMEM] * 3,
        out_specs=[VMEM] * len(offsets),
        compiler_params=params(16),
        cost_estimate=EARLY,
        name="more",
    )(features, send_rows, send_count)


def clear_map(map_ref):
    for cell in range(map_ref.shape[0]):
        map_ref[cell] = -1


def fill_map(ids_ref, live_ref, map_ref, first, count):
    for n in range(count):
        t = first + n
        map_ref[ids_ref[t]] = jnp.where(live_ref[t] > 0, t, -1)


def cell_tile(tiles_ref, map_ref, cell):
    slot = map_ref[cell]
    tile = tiles_ref[jnp.maximum(slot, 0)]
    return jnp.where(slot >= 0, tile, jnp.zeros_like(tile))


def edge_line(tiles_ref, map_ref, row, cols, sources, per):
    return [cell_tile(tiles_ref, map_ref, row * cols + source * per + j) for source in sources for j in range(per)]


def hub_line(adj_ref, live_ref, row, size, owner, per):
    line = []
    for b in [owner * per + j for j in range(per)]:
        cell = adj_ref[pl.ds(pl.multiple_of(row * size, size), size), pl.ds(pl.multiple_of(b * size, size), size)]
        line.append(jnp.where(live_ref[b, row] > 0, cell, jnp.zeros_like(cell)))
    return line


def local_kernel(block, feat_ref, send_ref, count_ref, tiles_ref, edge_ref, adj_ref, live_vmem, hub_ref, *refs):
    sources, (out_ref, map_hbm, core_ref, *refs) = refs[:4], refs[4:]
    *tables, live_ref, local_map, edge_map, rhs_ref, sems = refs
    copies = start_all([*sources, live_vmem], [*tables, live_ref], sems)
    shard = hub_ref.shape[0]
    own_ref = rhs_ref.at[shard:]
    rhs_ref[:shard, :] = hub_ref[...]
    gather_groups([(1,)], send_ref, count_ref, feat_ref, [core_ref])
    wait_all(copies)
    clear_map(local_map)
    fill_map(tables[0], tables[1], local_map, 0, tables[0].shape[0])
    clear_map(edge_map)
    gather_groups([(0,)], send_ref, count_ref, feat_ref, [own_ref])
    size = tiles_ref.shape[1]
    rows = feat_ref.shape[0]
    cols, edge_cols = rows // size, edge_map.shape[0] // (rows // size)
    steps = rows // (block * size)
    share = tables[2].shape[0] // steps

    def span(m):
        return pl.ds(pl.multiple_of(m * block * size, block * size), block * size)

    def local_body(m, _):
        blocks = []
        for i in range(block):
            row = m * block + i
            line = [cell_tile(tiles_ref, local_map, row * cols + j) for j in range(cols)]
            blocks.append(jnp.concatenate(line, axis=1))
        out_ref[span(m), :] = dot(jnp.concatenate(blocks, axis=0), feat_ref[...])
        fill_map(tables[2], tables[3], edge_map, m * share, share)
        return 0

    lax.fori_loop(0, steps, local_body, 0)
    fill_map(tables[2], tables[3], edge_map, steps * share, tables[2].shape[0] - steps * share)
    write = pltpu.make_async_copy(edge_map, map_hbm, sems.at[5])
    write.start()
    me, loop = lax.axis_index("row"), lax.axis_index("loop")
    per = own_ref.shape[0] // size

    def own_body(m, _):
        blocks = []
        for i in range(block):
            row = m * block + i
            line = hub_line(adj_ref, live_ref, row, size, loop, shard // size)
            line += edge_line(edge_ref, edge_map, row, edge_cols, [me], per)
            blocks.append(jnp.concatenate(line, axis=1))
        out_ref[span(m), :] += dot(jnp.concatenate(blocks, axis=0), rhs_ref[...])
        return 0

    lax.fori_loop(0, steps, own_body, 0)
    write.wait()


def local_term(features, send_rows, send_count, tables, tiles, edges, adj, hub_live, hub):
    rows, width = features.shape
    peers, slots = send_rows.shape
    size = tiles.shape[1]
    local_cells, edge_cells = (rows // size) ** 2, (rows // size) * (peers * slots // size)
    return pl.pallas_call(
        functools.partial(local_kernel, 8),
        out_shape=[
            jax.ShapeDtypeStruct(features.shape, F32),
            jax.ShapeDtypeStruct((edge_cells,), I32),
            jax.ShapeDtypeStruct((slots, width), BF),
        ],
        in_specs=[VMEM] * 8 + [HBM] * 4,
        out_specs=[VMEM, ANY, VMEM],
        scratch_shapes=[pltpu.SMEM(x.shape, I32) for x in tables]
        + [pltpu.SMEM(hub_live.shape, I32), pltpu.SMEM((local_cells,), I32), pltpu.SMEM((edge_cells,), I32)]
        + [pltpu.VMEM((hub.shape[0] + slots, width), BF), pltpu.SemaphoreType.DMA((6,))],
        compiler_params=params(16),
        cost_estimate=FREE,
        name="local",
    )(features, send_rows, send_count, tiles, edges, adj, hub_live, hub, *hbm(*tables))


def stack_kernel(rows, *refs):
    *array_refs, out_ref = refs
    at = 0
    for array_ref, (first, count) in zip(array_refs, rows):
        out_ref[at : at + count, :] = array_ref[first : first + count, :]
        at += count


def stack(rows, arrays):
    return pl.pallas_call(
        functools.partial(stack_kernel, rows),
        out_shape=jax.ShapeDtypeStruct((sum(count for _, count in rows), arrays[0].shape[1]), BF),
        in_specs=[VMEM] * len(arrays),
        out_specs=VMEM,
        compiler_params=params(16),
        cost_estimate=FREE,
        name="stack",
    )(*arrays)


def masked_line(adj_ref, mask_ref, row, size, columns):
    span = pl.ds(pl.multiple_of(row * size, size), size)
    line = []
    for column in columns:
        mask = jnp.broadcast_to(mask_ref[pl.ds(row, 1), column], (size, column.size)).astype(BF)
        line.append(adj_ref[span, column] * mask)
    return jnp.concatenate(line, axis=1)


def middle_kernel(block, hubs, pieces, map_ref, live_ref, adj_ref, edge_ref, acc_ref, *refs):
    *array_refs, out_ref, mask_ref, edge_map, hub_rhs, rhs_ref, sem = refs
    table = pltpu.make_async_copy(map_ref, edge_map, sem)
    table.start()
    me, loop = lax.axis_index("row"), lax.axis_index("loop")
    core = lax.rem(me, 2)
    tiles, rows = live_ref.shape
    size = adj_ref.shape[0] // rows
    cols = edge_map.shape[0] // rows
    shard, slots = hub_rhs.shape[0] // len(hubs), rhs_ref.shape[0] // len(pieces)
    columns = []
    for n, (even, odd) in enumerate(hubs):
        owner = loop ^ jnp.where(core == 0, even, odd)
        columns.append(pl.ds(pl.multiple_of(owner * shard, shard), shard))
        hub_rhs[n * shard : (n + 1) * shard, :] = array_refs[n][...]
    for n in range(len(pieces)):
        rhs_ref[n * slots : (n + 1) * slots, :] = array_refs[len(hubs) + n][:slots, :]
    sources = [me ^ offset for offset in pieces]
    lane = lax.broadcasted_iota(I32, (tiles, adj_ref.shape[1]), 1)
    first = lax.broadcasted_iota(I32, (tiles, adj_ref.shape[1]), 0) * size
    inside = (lane >= first) & (lane < first + size)
    live = live_ref[...]
    for row in range(rows):
        hit = jnp.where(inside & (live[:, row : row + 1] > 0), 1.0, 0.0)
        mask_ref[row : row + 1, :] = jnp.sum(hit, axis=0, keepdims=True)

    def span(m):
        return pl.ds(pl.multiple_of(m * block * size, block * size), block * size)

    def hub_body(m, _):
        blocks = [masked_line(adj_ref, mask_ref, m * block + i, size, columns) for i in range(block)]
        out_ref[span(m), :] = acc_ref[span(m), :] + dot(jnp.concatenate(blocks, axis=0), hub_rhs[...])
        return 0

    lax.fori_loop(0, rows // block, hub_body, 0)
    table.wait()

    def edge_body(m, _):
        lines = [
            edge_line(edge_ref, edge_map, m * block + i, cols, sources, slots // size) for i in range(block)
        ]
        found = jnp.concatenate([jnp.concatenate(line, axis=1) for line in lines], axis=0)
        out_ref[span(m), :] += dot(found, rhs_ref[...])
        return 0

    lax.fori_loop(0, rows // block, edge_body, 0)


def middle_term(hubs, pieces, slots, edge_map, hub_live, adj, edges, acc, arrays):
    shard, width = arrays[0].shape
    return pl.pallas_call(
        functools.partial(middle_kernel, 8, hubs, pieces),
        out_shape=[
            jax.ShapeDtypeStruct(acc.shape, F32),
            jax.ShapeDtypeStruct((hub_live.shape[1], adj.shape[1]), F32),
        ],
        in_specs=[ANY] + [VMEM] * (4 + len(arrays)),
        out_specs=[VMEM] * 2,
        scratch_shapes=[
            pltpu.SMEM(edge_map.shape, I32),
            pltpu.VMEM((len(hubs) * shard, width), BF),
            pltpu.VMEM((len(pieces) * slots, width), BF),
            pltpu.SemaphoreType.DMA,
        ],
        compiler_params=params(16),
        cost_estimate=FREE,
        name="middle",
    )(edge_map, hub_live, adj, edges, acc, *arrays)


def last_kernel(block, pieces, hubs, map_ref, edge_ref, adj_ref, mask_ref, acc_ref, weight_ref, *refs):
    *array_refs, out_ref, edge_map, hub_ref, rhs_ref, total_ref, stage_ref, sems = refs
    size = edge_ref.shape[1]
    rows = acc_ref.shape[0]
    steps = rows // (block * size)
    table = pltpu.make_async_copy(map_ref, edge_map, sems.at[steps])
    table.start()
    me, loop = lax.axis_index("row"), lax.axis_index("loop")
    core = lax.rem(me, 2)
    cols = edge_map.shape[0] // (rows // size)
    slots = rhs_ref.shape[0] // len(pieces)
    shard = hub_ref.shape[0] // len(hubs)
    columns = []
    for n, (array, first, even, odd) in enumerate(hubs):
        owner = loop ^ jnp.where(core == 0, even, odd)
        columns.append(pl.ds(pl.multiple_of(owner * shard, shard), shard))
        hub_ref[n * shard : (n + 1) * shard, :] = array_refs[array][first : first + shard, :]
    for n, (array, first, _) in enumerate(pieces):
        rhs_ref[n * slots : (n + 1) * slots, :] = array_refs[array][first : first + slots, :]
    sources = [me ^ offset for _, _, offset in pieces]

    def span(m):
        return pl.ds(pl.multiple_of(m * block * size, block * size), block * size)

    def write(m):
        return pltpu.make_async_copy(stage_ref.at[span(m)], out_ref.at[span(m)], sems.at[m])

    def hub_body(m, _):
        blocks = [masked_line(adj_ref, mask_ref, m * block + i, size, columns) for i in range(block)]
        total_ref[span(m), :] = acc_ref[span(m), :] + dot(jnp.concatenate(blocks, axis=0), hub_ref[...])
        return 0

    lax.fori_loop(0, steps, hub_body, 0)
    table.wait()

    def body(m, _):
        lines = [
            edge_line(edge_ref, edge_map, m * block + i, cols, sources, slots // size) for i in range(block)
        ]
        tiles = jnp.concatenate([jnp.concatenate(line, axis=1) for line in lines], axis=0)
        total = total_ref[span(m), :] + dot(tiles, rhs_ref[...])
        stage_ref[span(m), :] = jnp.maximum(dot(total.astype(BF), weight_ref[...]), 0.0).astype(BF)
        write(m).start()
        return 0

    lax.fori_loop(0, steps, body, 0)
    for m in range(steps):
        write(m).wait()


def last_term(pieces, hubs, slots, shard, edge_map, edges, adj, mask, acc, weight, arrays):
    block = 8
    rows, width = acc.shape
    return pl.pallas_call(
        functools.partial(last_kernel, block, pieces, hubs),
        out_shape=jax.ShapeDtypeStruct(acc.shape, BF),
        in_specs=[ANY] + [VMEM] * (5 + len(arrays)),
        out_specs=HBM,
        scratch_shapes=[
            pltpu.SMEM(edge_map.shape, I32),
            pltpu.VMEM((len(hubs) * shard, width), BF),
            pltpu.VMEM((len(pieces) * slots, width), BF),
            pltpu.VMEM(acc.shape, F32),
            pltpu.VMEM(acc.shape, BF),
            pltpu.SemaphoreType.DMA((rows // (block * edges.shape[1]) + 1,)),
        ],
        compiler_params=params(16),
        cost_estimate=FREE,
        name="last",
    )(edge_map, edges, adj, mask, acc, weight, *arrays)


def swap(x, axis, offset):
    return lax.ppermute(x, axis, [(i, i ^ offset) for i in range(lax.axis_size(axis))])


def swap_by_core(x, even, odd):
    peers, ring = lax.axis_size("row"), lax.axis_size("loop")
    pairs = [(r * ring + l, r * ring + (l ^ (odd if r % 2 else even))) for r in range(peers) for l in range(ring)]
    return lax.ppermute(x, ("row", "loop"), pairs)


def per_device(
    features,
    weight,
    local_tiles,
    local_ids,
    local_live,
    send_rows,
    send_count,
    edge_tiles,
    edge_ids,
    edge_live,
    hub_feats,
    hub_adj,
    hub_live,
):
    peers, ring = lax.axis_size("row"), lax.axis_size("loop")
    slots = send_rows.shape[2]
    size = local_tiles.shape[1]
    tile_rows = features.shape[0] // size
    chips = range(2, peers, 2)
    near_chips = [c for c in chips if c & (c - 1) == 0]
    far_chips = [c for c in chips if c not in near_chips]
    feat, sends, counts, hub, live, *packed = pack(
        [(c, c ^ 1) for c in far_chips], features, send_rows[0], send_count, hub_feats, hub_live.T
    )
    from_far = [swap(x, "row", c) for x, c in zip(packed, far_chips)]
    packed = pack_more([(c, c ^ 1) for c in near_chips], feat, sends, counts)
    from_near = [swap(x, "row", c) for x, c in zip(packed, near_chips)]
    near = swap(hub, "loop", 1)
    far = [swap_by_core(hub, offset, offset + 1) for offset in range(2, ring, 2)]
    acc, edge_map, to_core = local_term(
        feat,
        sends,
        counts,
        (local_ids, local_live, edge_ids, edge_live),
        local_tiles,
        edge_tiles,
        hub_adj,
        live,
        hub,
    )
    arrived = from_far + from_near
    shard = hub.shape[0]
    rows = [(0, slots)] + [(slots, slots)] * len(arrived) + [(0, shard)] * len(far)
    shared = swap(stack(rows, [to_core, *arrived, *far, near]), "row", 1)
    hubs = [(1, 1)] + [(2 * n + 2, 2 * n + 3) for n in range(len(far))]
    order = far_chips + near_chips
    acc, mask = middle_term(
        hubs, order, slots, edge_map, live, hub_adj, edge_tiles, acc, [near, *far, *arrived]
    )
    pieces = [(0, 0, 1)] + [(0, (1 + n) * slots, c ^ 1) for n, c in enumerate(order)]
    at = len(pieces) * slots
    hubs = [(0, at + n * shard, 2 * n + 3, 2 * n + 2) for n in range(len(far))]
    return last_term(pieces, hubs, slots, shard, edge_map, edge_tiles, hub_adj, mask, acc, weight, [shared])


def solution(mesh):
    both = ("row", "loop")
    placed = (
        P(both, None),
        P(),
        P(both, None, None),
        P(both),
        P(both),
        P(both, None, None),
        P(both, None),
        P(both, None, None),
        P(both),
        P(both),
        P("loop", None),
        P(both, None),
        P(both, None),
    )
    return jax.shard_map(per_device, mesh=mesh, in_specs=placed, out_specs=P(both, None), check_vma=False)
```

```python
import functools

import jax
import jax.numpy as jnp
from jax import lax
from jax.experimental import pallas as pl
from jax.experimental.pallas import tpu as pltpu
from jax.sharding import PartitionSpec as P

BF = jnp.bfloat16
F32 = jnp.float32
I32 = jnp.int32
EARLY = pl.CostEstimate(flops=1 << 35, bytes_accessed=0, transcendentals=0)
VMEM = pl.BlockSpec(memory_space=pltpu.VMEM)
SMEM = pl.BlockSpec(memory_space=pltpu.SMEM)
HBM = pl.BlockSpec(memory_space=pltpu.HBM)
ANY = pl.BlockSpec(memory_space=pl.ANY)
MIB = 1 << 20
FREE = pl.CostEstimate(flops=0, bytes_accessed=0, transcendentals=0)
VMEM = pl.BlockSpec(memory_space=pltpu.VMEM)
SMEM = pl.BlockSpec(memory_space=pltpu.SMEM)
HBM = pl.BlockSpec(memory_space=pltpu.HBM)
ANY = pl.BlockSpec(memory_space=pl.ANY)
MIB = 1 << 20
FREE = pl.CostEstimate(flops=0, bytes_accessed=0, transcendentals=0)
LONG = pl.CostEstimate(flops=1 << 35, bytes_accessed=0, transcendentals=0)


def params(mib):
    return pltpu.CompilerParams(vmem_limit_bytes=mib * MIB)


def hbm(*arrays):
    return [pltpu.with_memory_space_constraint(x, pltpu.HBM) for x in arrays]


def dot(a, b):
    return jnp.dot(a, b, preferred_element_type=F32)


def picks(send_ref, count_ref, rows, peer, scalar):
    slots = send_ref.shape[1]
    index = send_ref[pl.ds(peer, 1), :]
    slot = lax.broadcasted_iota(I32, (1, slots), 1)
    if scalar:
        count = count_ref[0, peer]
    else:
        peers = lax.broadcasted_iota(I32, count_ref.shape, 1)
        count = jnp.sum(jnp.where(peers == peer, count_ref[...], 0), axis=1, keepdims=True)
    index = jnp.where(slot < count, index, -1)
    lane = lax.broadcasted_iota(I32, (128, 128), 1)
    blocks = []
    for part in range(slots // 128):
        column = jnp.broadcast_to(index[:, part * 128 : (part + 1) * 128], (128, 128)).T
        line = [jnp.where(column == lane + c * 128, 1.0, 0.0).astype(BF) for c in range(rows // 128)]
        blocks.append(jnp.concatenate(line, axis=1))
    return jnp.concatenate(blocks, axis=0)


def gather_groups(offsets, send_ref, count_ref, feat_ref, packed, scalar=False):
    me = lax.axis_index("row")
    rows = feat_ref.shape[0]
    for out_ref, group in zip(packed, offsets):
        hot = [picks(send_ref, count_ref, rows, me ^ offset, scalar) for offset in group]
        out_ref[...] = dot(jnp.concatenate(hot, axis=0), feat_ref[...]).astype(BF)


def start_all(sources, targets, sems):
    copies = [pltpu.make_async_copy(x, y, sems.at[n]) for n, (x, y) in enumerate(zip(sources, targets))]
    for copy in copies:
        copy.start()
    return copies


def wait_all(copies):
    for copy in copies:
        copy.wait()


def pack_kernel(offsets, feat_hbm, send_hbm, count_hbm, hub_hbm, live_hbm, *refs):
    targets, (*packed, scalars, sems) = refs[:5], refs[5:]
    feat_ref, send_ref = targets[:2]
    sources = [feat_hbm, send_hbm, count_hbm, hub_hbm, live_hbm, count_hbm]
    copies = start_all(sources, [*targets, scalars], sems)
    wait_all(copies[:2] + copies[5:])
    gather_groups(offsets, send_ref, scalars, feat_ref, packed, scalar=True)
    wait_all(copies[2:5])


def pack(offsets, features, send_rows, send_count, hub_feats, hub_live):
    slots, width = send_rows.shape[1], features.shape[1]
    arrays = (features, send_rows, send_count, hub_feats, hub_live)
    return pl.pallas_call(
        functools.partial(pack_kernel, offsets),
        out_shape=[jax.ShapeDtypeStruct(x.shape, x.dtype) for x in arrays]
        + [jax.ShapeDtypeStruct((len(group) * slots, width), BF) for group in offsets],
        in_specs=[HBM] * 5,
        out_specs=[VMEM] * (5 + len(offsets)),
        scratch_shapes=[pltpu.SMEM(send_count.shape, I32), pltpu.SemaphoreType.DMA((6,))],
        compiler_params=params(16),
        cost_estimate=FREE,
        name="pack",
    )(*hbm(*arrays))


def more_kernel(offsets, feat_ref, send_ref, count_ref, *packed):
    gather_groups(offsets, send_ref, count_ref, feat_ref, packed)


def pack_more(offsets, features, send_rows, send_count):
    slots, width = send_rows.shape[1], features.shape[1]
    return pl.pallas_call(
        functools.partial(more_kernel, offsets),
        out_shape=[jax.ShapeDtypeStruct((len(group) * slots, width), BF) for group in offsets],
        in_specs=[VMEM] * 3,
        out_specs=[VMEM] * len(offsets),
        compiler_params=params(16),
        cost_estimate=EARLY,
        name="more",
    )(features, send_rows, send_count)


def clear_map(map_ref):
    for cell in range(map_ref.shape[0]):
        map_ref[cell] = -1


def fill_map(ids_ref, live_ref, map_ref, first, count):
    for n in range(count):
        t = first + n
        map_ref[ids_ref[t]] = jnp.where(live_ref[t] > 0, t, -1)


def cell_tile(tiles_ref, map_ref, cell):
    slot = map_ref[cell]
    tile = tiles_ref[jnp.maximum(slot, 0)]
    return jnp.where(slot >= 0, tile, jnp.zeros_like(tile))


def edge_line(tiles_ref, map_ref, row, cols, sources, per):
    return [cell_tile(tiles_ref, map_ref, row * cols + source * per + j) for source in sources for j in range(per)]


def hub_line(adj_ref, live_ref, row, size, owner, per):
    line = []
    for b in [owner * per + j for j in range(per)]:
        cell = adj_ref[pl.ds(pl.multiple_of(row * size, size), size), pl.ds(pl.multiple_of(b * size, size), size)]
        line.append(jnp.where(live_ref[b, row] > 0, cell, jnp.zeros_like(cell)))
    return line


def local_kernel(block, feat_ref, send_ref, count_ref, tiles_ref, edge_ref, adj_ref, live_vmem, hub_ref, *refs):
    sources, (out_ref, map_hbm, core_ref, mask_ref, *refs) = refs[:4], refs[4:]
    *tables, live_ref, local_map, edge_map, rhs_ref, sems = refs
    copies = start_all([*sources, live_vmem], [*tables, live_ref], sems)
    shard = hub_ref.shape[0]
    own_ref = rhs_ref.at[shard:]
    rhs_ref[:shard, :] = hub_ref[...]
    gather_groups([(1,)], send_ref, count_ref, feat_ref, [core_ref])
    wait_all(copies)
    clear_map(local_map)
    fill_map(tables[0], tables[1], local_map, 0, tables[0].shape[0])
    clear_map(edge_map)
    gather_groups([(0,)], send_ref, count_ref, feat_ref, [own_ref])
    size = tiles_ref.shape[1]
    rows = feat_ref.shape[0]
    cols, edge_cols = rows // size, edge_map.shape[0] // (rows // size)
    steps = rows // (block * size)
    share = tables[2].shape[0] // steps

    def span(m):
        return pl.ds(pl.multiple_of(m * block * size, block * size), block * size)

    def local_body(m, _):
        blocks = []
        for i in range(block):
            row = m * block + i
            line = [cell_tile(tiles_ref, local_map, row * cols + j) for j in range(cols)]
            blocks.append(jnp.concatenate(line, axis=1))
        out_ref[span(m), :] = dot(jnp.concatenate(blocks, axis=0), feat_ref[...])
        fill_map(tables[2], tables[3], edge_map, m * share, share)
        for i in range(block):
            row = m * block + i
            hit = jnp.sum(jnp.where(at_row == row, live_vmem[...], 0), axis=1, keepdims=True)
            mask_ref[pl.ds(row, 1), :] = jnp.sum(jnp.where(inside & (hit > 0), 1.0, 0.0), axis=0, keepdims=True)
        return 0

    at_row = lax.broadcasted_iota(I32, live_vmem.shape, 1)
    cells = (live_vmem.shape[0], adj_ref.shape[1])
    lane, first = lax.broadcasted_iota(I32, cells, 1), lax.broadcasted_iota(I32, cells, 0) * size
    inside = (lane >= first) & (lane < first + size)

    lax.fori_loop(0, steps, local_body, 0)
    fill_map(tables[2], tables[3], edge_map, steps * share, tables[2].shape[0] - steps * share)
    write = pltpu.make_async_copy(edge_map, map_hbm, sems.at[5])
    write.start()
    me, loop = lax.axis_index("row"), lax.axis_index("loop")
    per = own_ref.shape[0] // size

    def own_body(m, _):
        blocks = []
        for i in range(block):
            row = m * block + i
            line = hub_line(adj_ref, live_ref, row, size, loop, shard // size)
            line += edge_line(edge_ref, edge_map, row, edge_cols, [me], per)
            blocks.append(jnp.concatenate(line, axis=1))
        out_ref[span(m), :] += dot(jnp.concatenate(blocks, axis=0), rhs_ref[...])
        return 0

    lax.fori_loop(0, steps, own_body, 0)
    write.wait()


def local_term(features, send_rows, send_count, tables, tiles, edges, adj, hub_live, hub):
    rows, width = features.shape
    peers, slots = send_rows.shape
    size = tiles.shape[1]
    local_cells, edge_cells = (rows // size) ** 2, (rows // size) * (peers * slots // size)
    return pl.pallas_call(
        functools.partial(local_kernel, 8),
        out_shape=[
            jax.ShapeDtypeStruct(features.shape, F32),
            jax.ShapeDtypeStruct((edge_cells,), I32),
            jax.ShapeDtypeStruct((slots, width), BF),
            jax.ShapeDtypeStruct((rows // size, adj.shape[1]), F32),
        ],
        in_specs=[VMEM] * 8 + [HBM] * 4,
        out_specs=[VMEM, ANY, VMEM, VMEM],
        scratch_shapes=[pltpu.SMEM(x.shape, I32) for x in tables]
        + [pltpu.SMEM(hub_live.shape, I32), pltpu.SMEM((local_cells,), I32), pltpu.SMEM((edge_cells,), I32)]
        + [pltpu.VMEM((hub.shape[0] + slots, width), BF), pltpu.SemaphoreType.DMA((6,))],
        compiler_params=params(16),
        cost_estimate=FREE,
        name="local",
    )(features, send_rows, send_count, tiles, edges, adj, hub_live, hub, *hbm(*tables))


def stack_kernel(rows, *refs):
    *array_refs, out_ref = refs
    at = 0
    for array_ref, (first, count) in zip(array_refs, rows):
        out_ref[at : at + count, :] = array_ref[first : first + count, :]
        at += count


def stack(rows, arrays):
    return pl.pallas_call(
        functools.partial(stack_kernel, rows),
        out_shape=jax.ShapeDtypeStruct((sum(count for _, count in rows), arrays[0].shape[1]), BF),
        in_specs=[VMEM] * len(arrays),
        out_specs=VMEM,
        compiler_params=params(16),
        cost_estimate=FREE,
        name="stack",
    )(*arrays)


def masked_line(adj_ref, mask_ref, row, size, columns):
    span = pl.ds(pl.multiple_of(row * size, size), size)
    line = []
    for column in columns:
        mask = jnp.broadcast_to(mask_ref[pl.ds(row, 1), column], (size, column.size)).astype(BF)
        line.append(adj_ref[span, column] * mask)
    return jnp.concatenate(line, axis=1)


def middle_kernel(block, hubs, pieces, map_ref, mask_ref, adj_ref, edge_ref, acc_ref, *refs):
    *array_refs, out_ref, edge_map, hub_rhs, rhs_ref, sem = refs
    table = pltpu.make_async_copy(map_ref, edge_map, sem)
    table.start()
    me, loop = lax.axis_index("row"), lax.axis_index("loop")
    core = lax.rem(me, 2)
    rows = mask_ref.shape[0]
    size = adj_ref.shape[0] // rows
    cols = edge_map.shape[0] // rows
    shard, slots = hub_rhs.shape[0] // len(hubs), rhs_ref.shape[0] // len(pieces)
    columns = []
    for n, (even, odd) in enumerate(hubs):
        owner = loop ^ jnp.where(core == 0, even, odd)
        columns.append(pl.ds(pl.multiple_of(owner * shard, shard), shard))
        hub_rhs[n * shard : (n + 1) * shard, :] = array_refs[n][...]
    for n in range(len(pieces)):
        rhs_ref[n * slots : (n + 1) * slots, :] = array_refs[len(hubs) + n][:slots, :]
    sources = [me ^ offset for offset in pieces]
    def span(m):
        return pl.ds(pl.multiple_of(m * block * size, block * size), block * size)

    def hub_body(m, _):
        blocks = [masked_line(adj_ref, mask_ref, m * block + i, size, columns) for i in range(block)]
        out_ref[span(m), :] = acc_ref[span(m), :] + dot(jnp.concatenate(blocks, axis=0), hub_rhs[...])
        return 0

    lax.fori_loop(0, rows // block, hub_body, 0)
    table.wait()

    def edge_body(m, _):
        lines = [
            edge_line(edge_ref, edge_map, m * block + i, cols, sources, slots // size) for i in range(block)
        ]
        found = jnp.concatenate([jnp.concatenate(line, axis=1) for line in lines], axis=0)
        out_ref[span(m), :] += dot(found, rhs_ref[...])
        return 0

    lax.fori_loop(0, rows // block, edge_body, 0)


def middle_term(hubs, pieces, slots, edge_map, mask, adj, edges, acc, arrays):
    shard, width = arrays[0].shape
    return pl.pallas_call(
        functools.partial(middle_kernel, 8, hubs, pieces),
        out_shape=jax.ShapeDtypeStruct(acc.shape, F32),
        in_specs=[ANY] + [VMEM] * (4 + len(arrays)),
        out_specs=VMEM,
        scratch_shapes=[
            pltpu.SMEM(edge_map.shape, I32),
            pltpu.VMEM((len(hubs) * shard, width), BF),
            pltpu.VMEM((len(pieces) * slots, width), BF),
            pltpu.SemaphoreType.DMA,
        ],
        compiler_params=params(16),
        cost_estimate=FREE,
        name="middle",
    )(edge_map, mask, adj, edges, acc, *arrays)


def last_kernel(block, pieces, hubs, map_ref, edge_ref, adj_ref, mask_ref, acc_ref, weight_ref, *refs):
    *array_refs, out_ref, edge_map, hub_ref, rhs_ref, total_ref, stage_ref, sems = refs
    size = edge_ref.shape[1]
    rows = acc_ref.shape[0]
    steps = rows // (block * size)
    table = pltpu.make_async_copy(map_ref, edge_map, sems.at[steps])
    table.start()
    me, loop = lax.axis_index("row"), lax.axis_index("loop")
    core = lax.rem(me, 2)
    cols = edge_map.shape[0] // (rows // size)
    slots = rhs_ref.shape[0] // len(pieces)
    shard = hub_ref.shape[0] // len(hubs)
    columns = []
    for n, (array, first, even, odd) in enumerate(hubs):
        owner = loop ^ jnp.where(core == 0, even, odd)
        columns.append(pl.ds(pl.multiple_of(owner * shard, shard), shard))
        hub_ref[n * shard : (n + 1) * shard, :] = array_refs[array][first : first + shard, :]
    for n, (array, first, _) in enumerate(pieces):
        rhs_ref[n * slots : (n + 1) * slots, :] = array_refs[array][first : first + slots, :]
    sources = [me ^ offset for _, _, offset in pieces]

    def span(m):
        return pl.ds(pl.multiple_of(m * block * size, block * size), block * size)

    def write(m):
        return pltpu.make_async_copy(stage_ref.at[span(m)], out_ref.at[span(m)], sems.at[m])

    def hub_body(m, _):
        blocks = [masked_line(adj_ref, mask_ref, m * block + i, size, columns) for i in range(block)]
        total_ref[span(m), :] = acc_ref[span(m), :] + dot(jnp.concatenate(blocks, axis=0), hub_ref[...])
        return 0

    lax.fori_loop(0, steps, hub_body, 0)
    table.wait()

    def body(m, _):
        lines = [
            edge_line(edge_ref, edge_map, m * block + i, cols, sources, slots // size) for i in range(block)
        ]
        tiles = jnp.concatenate([jnp.concatenate(line, axis=1) for line in lines], axis=0)
        total = total_ref[span(m), :] + dot(tiles, rhs_ref[...])
        stage_ref[span(m), :] = jnp.maximum(dot(total.astype(BF), weight_ref[...]), 0.0).astype(BF)
        write(m).start()
        return 0

    lax.fori_loop(0, steps, body, 0)
    for m in range(steps):
        write(m).wait()


def last_term(pieces, hubs, slots, shard, edge_map, edges, adj, mask, acc, weight, arrays):
    block = 8
    rows, width = acc.shape
    return pl.pallas_call(
        functools.partial(last_kernel, block, pieces, hubs),
        out_shape=jax.ShapeDtypeStruct(acc.shape, BF),
        in_specs=[ANY] + [VMEM] * (5 + len(arrays)),
        out_specs=HBM,
        scratch_shapes=[
            pltpu.SMEM(edge_map.shape, I32),
            pltpu.VMEM((len(hubs) * shard, width), BF),
            pltpu.VMEM((len(pieces) * slots, width), BF),
            pltpu.VMEM(acc.shape, F32),
            pltpu.VMEM(acc.shape, BF),
            pltpu.SemaphoreType.DMA((rows // (block * edges.shape[1]) + 1,)),
        ],
        compiler_params=params(16),
        cost_estimate=FREE,
        name="last",
    )(edge_map, edges, adj, mask, acc, weight, *arrays)


def swap(x, axis, offset):
    return lax.ppermute(x, axis, [(i, i ^ offset) for i in range(lax.axis_size(axis))])


def swap_by_core(x, even, odd):
    peers, ring = lax.axis_size("row"), lax.axis_size("loop")
    pairs = [(r * ring + l, r * ring + (l ^ (odd if r % 2 else even))) for r in range(peers) for l in range(ring)]
    return lax.ppermute(x, ("row", "loop"), pairs)


def per_device(
    features,
    weight,
    local_tiles,
    local_ids,
    local_live,
    send_rows,
    send_count,
    edge_tiles,
    edge_ids,
    edge_live,
    hub_feats,
    hub_adj,
    hub_live,
):
    peers, ring = lax.axis_size("row"), lax.axis_size("loop")
    slots = send_rows.shape[2]
    size = local_tiles.shape[1]
    tile_rows = features.shape[0] // size
    chips = range(2, peers, 2)
    near_chips = [c for c in chips if c & (c - 1) == 0]
    far_chips = [c for c in chips if c not in near_chips]
    feat, sends, counts, hub, live, *packed = pack(
        [(c, c ^ 1) for c in far_chips], features, send_rows[0], send_count, hub_feats, hub_live.T
    )
    from_far = [swap(x, "row", c) for x, c in zip(packed, far_chips)]
    packed = pack_more([(c, c ^ 1) for c in near_chips], feat, sends, counts)
    from_near = [swap(x, "row", c) for x, c in zip(packed, near_chips)]
    near = swap(hub, "loop", 1)
    far = [swap_by_core(hub, offset, offset + 1) for offset in range(2, ring, 2)]
    acc, edge_map, to_core, mask = local_term(
        feat,
        sends,
        counts,
        (local_ids, local_live, edge_ids, edge_live),
        local_tiles,
        edge_tiles,
        hub_adj,
        live,
        hub,
    )
    arrived = from_far + from_near
    shard = hub.shape[0]
    rows = [(0, slots)] + [(slots, slots)] * len(arrived) + [(0, shard)] * len(far)
    shared = swap(stack(rows, [to_core, *arrived, *far, near]), "row", 1)
    hubs = [(1, 1)] + [(2 * n + 2, 2 * n + 3) for n in range(len(far))]
    order = far_chips + near_chips
    acc = middle_term(
        hubs, order, slots, edge_map, mask, hub_adj, edge_tiles, acc, [near, *far, *arrived]
    )
    pieces = [(0, 0, 1)] + [(0, (1 + n) * slots, c ^ 1) for n, c in enumerate(order)]
    at = len(pieces) * slots
    hubs = [(0, at + n * shard, 2 * n + 3, 2 * n + 2) for n in range(len(far))]
    return last_term(pieces, hubs, slots, shard, edge_map, edge_tiles, hub_adj, mask, acc, weight, [shared])


def solution(mesh):
    both = ("row", "loop")
    placed = (
        P(both, None),
        P(),
        P(both, None, None),
        P(both),
        P(both),
        P(both, None, None),
        P(both, None),
        P(both, None, None),
        P(both),
        P(both),
        P("loop", None),
        P(both, None),
        P(both, None),
    )
    return jax.shard_map(per_device, mesh=mesh, in_specs=placed, out_specs=P(both, None), check_vma=False)
```

```python
import functools

import jax
import jax.numpy as jnp
from jax import lax
from jax.experimental import pallas as pl
from jax.experimental.pallas import tpu as pltpu
from jax.sharding import PartitionSpec as P

BF = jnp.bfloat16
F32 = jnp.float32
I32 = jnp.int32
EARLY = pl.CostEstimate(flops=1 << 35, bytes_accessed=0, transcendentals=0)
VMEM = pl.BlockSpec(memory_space=pltpu.VMEM)
SMEM = pl.BlockSpec(memory_space=pltpu.SMEM)
HBM = pl.BlockSpec(memory_space=pltpu.HBM)
ANY = pl.BlockSpec(memory_space=pl.ANY)
MIB = 1 << 20
FREE = pl.CostEstimate(flops=0, bytes_accessed=0, transcendentals=0)


def params(mib):
    return pltpu.CompilerParams(vmem_limit_bytes=mib * MIB)


def hbm(*arrays):
    return [pltpu.with_memory_space_constraint(x, pltpu.HBM) for x in arrays]


def dot(a, b):
    return jnp.dot(a, b, preferred_element_type=F32)


def picks(send_ref, count_ref, rows, peer, scalar):
    slots = send_ref.shape[1]
    index = send_ref[pl.ds(peer, 1), :]
    slot = lax.broadcasted_iota(I32, (1, slots), 1)
    if scalar:
        count = count_ref[0, peer]
    else:
        peers = lax.broadcasted_iota(I32, count_ref.shape, 1)
        count = jnp.sum(jnp.where(peers == peer, count_ref[...], 0), axis=1, keepdims=True)
    index = jnp.where(slot < count, index, -1)
    lane = lax.broadcasted_iota(I32, (128, 128), 1)
    blocks = []
    for part in range(slots // 128):
        column = jnp.broadcast_to(index[:, part * 128 : (part + 1) * 128], (128, 128)).T
        line = [jnp.where(column == lane + c * 128, 1.0, 0.0).astype(BF) for c in range(rows // 128)]
        blocks.append(jnp.concatenate(line, axis=1))
    return jnp.concatenate(blocks, axis=0)


def gather_groups(offsets, send_ref, count_ref, feat_ref, packed, scalar=False):
    me = lax.axis_index("row")
    rows = feat_ref.shape[0]
    for out_ref, group in zip(packed, offsets):
        hot = [picks(send_ref, count_ref, rows, me ^ offset, scalar) for offset in group]
        out_ref[...] = dot(jnp.concatenate(hot, axis=0), feat_ref[...]).astype(BF)


def start_all(sources, targets, sems):
    copies = [pltpu.make_async_copy(x, y, sems.at[n]) for n, (x, y) in enumerate(zip(sources, targets))]
    for copy in copies:
        copy.start()
    return copies


def wait_all(copies):
    for copy in copies:
        copy.wait()


def pack_kernel(offsets, feat_hbm, send_hbm, count_hbm, hub_hbm, live_hbm, *refs):
    targets, (*packed, scalars, sems) = refs[:5], refs[5:]
    feat_ref, send_ref = targets[:2]
    sources = [feat_hbm, send_hbm, count_hbm, hub_hbm, live_hbm, count_hbm]
    copies = start_all(sources, [*targets, scalars], sems)
    wait_all(copies[:2] + copies[5:])
    gather_groups(offsets, send_ref, scalars, feat_ref, packed, scalar=True)
    wait_all(copies[2:5])


def pack(offsets, features, send_rows, send_count, hub_feats, hub_live):
    slots, width = send_rows.shape[1], features.shape[1]
    arrays = (features, send_rows, send_count, hub_feats, hub_live)
    return pl.pallas_call(
        functools.partial(pack_kernel, offsets),
        out_shape=[jax.ShapeDtypeStruct(x.shape, x.dtype) for x in arrays]
        + [jax.ShapeDtypeStruct((len(group) * slots, width), BF) for group in offsets],
        in_specs=[HBM] * 5,
        out_specs=[VMEM] * (5 + len(offsets)),
        scratch_shapes=[pltpu.SMEM(send_count.shape, I32), pltpu.SemaphoreType.DMA((6,))],
        compiler_params=params(16),
        cost_estimate=FREE,
        name="pack",
    )(*hbm(*arrays))


def more_kernel(offsets, feat_ref, send_ref, count_ref, *packed):
    gather_groups(offsets, send_ref, count_ref, feat_ref, packed)


def pack_more(offsets, features, send_rows, send_count):
    slots, width = send_rows.shape[1], features.shape[1]
    return pl.pallas_call(
        functools.partial(more_kernel, offsets),
        out_shape=[jax.ShapeDtypeStruct((len(group) * slots, width), BF) for group in offsets],
        in_specs=[VMEM] * 3,
        out_specs=[VMEM] * len(offsets),
        compiler_params=params(16),
        cost_estimate=EARLY,
        name="more",
    )(features, send_rows, send_count)


def clear_map(map_ref):
    for cell in range(map_ref.shape[0]):
        map_ref[cell] = -1


def fill_map(ids_ref, live_ref, map_ref, first, count):
    for n in range(count):
        t = first + n
        map_ref[ids_ref[t]] = jnp.where(live_ref[t] > 0, t, -1)


def cell_tile(tiles_ref, map_ref, cell):
    slot = map_ref[cell]
    tile = tiles_ref[jnp.maximum(slot, 0)]
    return jnp.where(slot >= 0, tile, jnp.zeros_like(tile))


def edge_line(tiles_ref, map_ref, row, cols, sources, per):
    return [cell_tile(tiles_ref, map_ref, row * cols + source * per + j) for source in sources for j in range(per)]


def hub_line(adj_ref, live_ref, row, size, owner, per):
    line = []
    for b in [owner * per + j for j in range(per)]:
        cell = adj_ref[pl.ds(pl.multiple_of(row * size, size), size), pl.ds(pl.multiple_of(b * size, size), size)]
        line.append(jnp.where(live_ref[b, row] > 0, cell, jnp.zeros_like(cell)))
    return line


def local_kernel(block, feat_ref, send_ref, count_ref, tiles_ref, edge_ref, adj_ref, live_vmem, hub_ref, *refs):
    sources, (out_ref, map_hbm, core_ref, mask_ref, *refs) = refs[:4], refs[4:]
    *tables, live_ref, local_map, edge_map, rhs_ref, sems = refs
    copies = start_all([*sources, live_vmem], [*tables, live_ref], sems)
    shard = hub_ref.shape[0]
    own_ref = rhs_ref.at[shard:]
    rhs_ref[:shard, :] = hub_ref[...]
    gather_groups([(1,)], send_ref, count_ref, feat_ref, [core_ref])
    wait_all(copies)
    clear_map(local_map)
    fill_map(tables[0], tables[1], local_map, 0, tables[0].shape[0])
    clear_map(edge_map)
    gather_groups([(0,)], send_ref, count_ref, feat_ref, [own_ref])
    size = tiles_ref.shape[1]
    rows = feat_ref.shape[0]
    cols, edge_cols = rows // size, edge_map.shape[0] // (rows // size)
    steps = rows // (block * size)
    share = tables[2].shape[0] // steps

    def span(m):
        return pl.ds(pl.multiple_of(m * block * size, block * size), block * size)

    def local_body(m, _):
        blocks = []
        for i in range(block):
            row = m * block + i
            line = [cell_tile(tiles_ref, local_map, row * cols + j) for j in range(cols)]
            blocks.append(jnp.concatenate(line, axis=1))
        out_ref[span(m), :] = dot(jnp.concatenate(blocks, axis=0), feat_ref[...])
        fill_map(tables[2], tables[3], edge_map, m * share, share)
        for i in range(block):
            row = m * block + i
            hit = jnp.sum(jnp.where(at_row == row, live_vmem[...], 0), axis=1, keepdims=True)
            mask_ref[pl.ds(row, 1), :] = jnp.sum(jnp.where(inside & (hit > 0), 1.0, 0.0), axis=0, keepdims=True)
        return 0

    at_row = lax.broadcasted_iota(I32, live_vmem.shape, 1)
    cells = (live_vmem.shape[0], adj_ref.shape[1])
    lane, first = lax.broadcasted_iota(I32, cells, 1), lax.broadcasted_iota(I32, cells, 0) * size
    inside = (lane >= first) & (lane < first + size)

    lax.fori_loop(0, steps, local_body, 0)
    fill_map(tables[2], tables[3], edge_map, steps * share, tables[2].shape[0] - steps * share)
    write = pltpu.make_async_copy(edge_map, map_hbm, sems.at[5])
    write.start()
    me, loop = lax.axis_index("row"), lax.axis_index("loop")
    per = own_ref.shape[0] // size

    def own_body(m, _):
        blocks = []
        for i in range(block):
            row = m * block + i
            line = hub_line(adj_ref, live_ref, row, size, loop, shard // size)
            line += edge_line(edge_ref, edge_map, row, edge_cols, [me], per)
            blocks.append(jnp.concatenate(line, axis=1))
        out_ref[span(m), :] += dot(jnp.concatenate(blocks, axis=0), rhs_ref[...])
        return 0

    lax.fori_loop(0, steps, own_body, 0)
    write.wait()


def local_term(features, send_rows, send_count, tables, tiles, edges, adj, hub_live, hub):
    rows, width = features.shape
    peers, slots = send_rows.shape
    size = tiles.shape[1]
    local_cells, edge_cells = (rows // size) ** 2, (rows // size) * (peers * slots // size)
    return pl.pallas_call(
        functools.partial(local_kernel, 8),
        out_shape=[
            jax.ShapeDtypeStruct(features.shape, F32),
            jax.ShapeDtypeStruct((edge_cells,), I32),
            jax.ShapeDtypeStruct((slots, width), BF),
            jax.ShapeDtypeStruct((rows // size, adj.shape[1]), F32),
        ],
        in_specs=[VMEM] * 8 + [HBM] * 4,
        out_specs=[VMEM, ANY, VMEM, VMEM],
        scratch_shapes=[pltpu.SMEM(x.shape, I32) for x in tables]
        + [pltpu.SMEM(hub_live.shape, I32), pltpu.SMEM((local_cells,), I32), pltpu.SMEM((edge_cells,), I32)]
        + [pltpu.VMEM((hub.shape[0] + slots, width), BF), pltpu.SemaphoreType.DMA((6,))],
        compiler_params=params(16),
        cost_estimate=FREE,
        name="local",
    )(features, send_rows, send_count, tiles, edges, adj, hub_live, hub, *hbm(*tables))


def stack_kernel(rows, *refs):
    *array_refs, out_ref = refs
    at = 0
    for array_ref, (first, count) in zip(array_refs, rows):
        out_ref[at : at + count, :] = array_ref[first : first + count, :]
        at += count


def stack(rows, arrays):
    return pl.pallas_call(
        functools.partial(stack_kernel, rows),
        out_shape=jax.ShapeDtypeStruct((sum(count for _, count in rows), arrays[0].shape[1]), BF),
        in_specs=[VMEM] * len(arrays),
        out_specs=VMEM,
        compiler_params=params(16),
        cost_estimate=FREE,
        name="stack",
    )(*arrays)


def masked_line(adj_ref, mask_ref, row, size, columns):
    span = pl.ds(pl.multiple_of(row * size, size), size)
    line = []
    for column in columns:
        mask = jnp.broadcast_to(mask_ref[pl.ds(row, 1), column], (size, column.size)).astype(BF)
        line.append(adj_ref[span, column] * mask)
    return jnp.concatenate(line, axis=1)


def middle_kernel(block, hubs, pieces, map_ref, mask_ref, adj_ref, edge_ref, acc_ref, *refs):
    *array_refs, out_ref, edge_map, hub_rhs, rhs_ref, sem = refs
    table = pltpu.make_async_copy(map_ref, edge_map, sem)
    table.start()
    me, loop = lax.axis_index("row"), lax.axis_index("loop")
    core = lax.rem(me, 2)
    rows = mask_ref.shape[0]
    size = adj_ref.shape[0] // rows
    cols = edge_map.shape[0] // rows
    shard, slots = hub_rhs.shape[0] // len(hubs), rhs_ref.shape[0] // len(pieces)
    columns = []
    for n, (even, odd) in enumerate(hubs):
        owner = loop ^ jnp.where(core == 0, even, odd)
        columns.append(pl.ds(pl.multiple_of(owner * shard, shard), shard))
        hub_rhs[n * shard : (n + 1) * shard, :] = array_refs[n][...]
    for n in range(len(pieces)):
        rhs_ref[n * slots : (n + 1) * slots, :] = array_refs[len(hubs) + n][:slots, :]
    sources = [me ^ offset for offset in pieces]
    def span(m):
        return pl.ds(pl.multiple_of(m * block * size, block * size), block * size)

    def hub_body(m, _):
        blocks = [masked_line(adj_ref, mask_ref, m * block + i, size, columns) for i in range(block)]
        out_ref[span(m), :] = acc_ref[span(m), :] + dot(jnp.concatenate(blocks, axis=0), hub_rhs[...])
        return 0

    lax.fori_loop(0, rows // block, hub_body, 0)
    table.wait()

    lines = [edge_line(edge_ref, edge_map, row, cols, sources, slots // size) for row in range(rows)]
    found = jnp.concatenate([jnp.concatenate(line, axis=1) for line in lines], axis=0)
    out_ref[...] += dot(found, rhs_ref[...])


def middle_term(hubs, pieces, slots, edge_map, mask, adj, edges, acc, arrays):
    shard, width = arrays[0].shape
    return pl.pallas_call(
        functools.partial(middle_kernel, 8, hubs, pieces),
        out_shape=jax.ShapeDtypeStruct(acc.shape, F32),
        in_specs=[ANY] + [VMEM] * (4 + len(arrays)),
        out_specs=VMEM,
        scratch_shapes=[
            pltpu.SMEM(edge_map.shape, I32),
            pltpu.VMEM((len(hubs) * shard, width), BF),
            pltpu.VMEM((len(pieces) * slots, width), BF),
            pltpu.SemaphoreType.DMA,
        ],
        compiler_params=params(16),
        cost_estimate=FREE,
        name="middle",
    )(edge_map, mask, adj, edges, acc, *arrays)


def last_kernel(block, pieces, hubs, map_ref, edge_ref, adj_ref, mask_ref, acc_ref, weight_ref, *refs):
    *array_refs, out_ref, edge_map, hub_ref, rhs_ref, total_ref, stage_ref, sems = refs
    size = edge_ref.shape[1]
    rows = acc_ref.shape[0]
    steps = rows // (block * size)
    table = pltpu.make_async_copy(map_ref, edge_map, sems.at[steps])
    table.start()
    me, loop = lax.axis_index("row"), lax.axis_index("loop")
    core = lax.rem(me, 2)
    cols = edge_map.shape[0] // (rows // size)
    slots = rhs_ref.shape[0] // len(pieces)
    shard = hub_ref.shape[0] // len(hubs)
    columns = []
    for n, (array, first, even, odd) in enumerate(hubs):
        owner = loop ^ jnp.where(core == 0, even, odd)
        columns.append(pl.ds(pl.multiple_of(owner * shard, shard), shard))
        hub_ref[n * shard : (n + 1) * shard, :] = array_refs[array][first : first + shard, :]
    for n, (array, first, _) in enumerate(pieces):
        rhs_ref[n * slots : (n + 1) * slots, :] = array_refs[array][first : first + slots, :]
    sources = [me ^ offset for _, _, offset in pieces]

    def span(m):
        return pl.ds(pl.multiple_of(m * block * size, block * size), block * size)

    def write(m):
        return pltpu.make_async_copy(stage_ref.at[span(m)], out_ref.at[span(m)], sems.at[m])

    def hub_body(m, _):
        blocks = [masked_line(adj_ref, mask_ref, m * block + i, size, columns) for i in range(block)]
        total_ref[span(m), :] = acc_ref[span(m), :] + dot(jnp.concatenate(blocks, axis=0), hub_ref[...])
        return 0

    lax.fori_loop(0, steps, hub_body, 0)
    table.wait()

    lines = [edge_line(edge_ref, edge_map, row, cols, sources, slots // size) for row in range(rows // size)]
    tiles = jnp.concatenate([jnp.concatenate(line, axis=1) for line in lines], axis=0)
    total_ref[...] += dot(tiles, rhs_ref[...])
    for m in range(steps):
        stage_ref[span(m), :] = jnp.maximum(dot(total_ref[span(m), :].astype(BF), weight_ref[...]), 0.0).astype(BF)
        write(m).start()
    for m in range(steps):
        write(m).wait()


def last_term(pieces, hubs, slots, shard, edge_map, edges, adj, mask, acc, weight, arrays):
    block = 8
    rows, width = acc.shape
    return pl.pallas_call(
        functools.partial(last_kernel, block, pieces, hubs),
        out_shape=jax.ShapeDtypeStruct(acc.shape, BF),
        in_specs=[ANY] + [VMEM] * (5 + len(arrays)),
        out_specs=HBM,
        scratch_shapes=[
            pltpu.SMEM(edge_map.shape, I32),
            pltpu.VMEM((len(hubs) * shard, width), BF),
            pltpu.VMEM((len(pieces) * slots, width), BF),
            pltpu.VMEM(acc.shape, F32),
            pltpu.VMEM(acc.shape, BF),
            pltpu.SemaphoreType.DMA((rows // (block * edges.shape[1]) + 1,)),
        ],
        compiler_params=params(16),
        cost_estimate=FREE,
        name="last",
    )(edge_map, edges, adj, mask, acc, weight, *arrays)


def swap(x, axis, offset):
    return lax.ppermute(x, axis, [(i, i ^ offset) for i in range(lax.axis_size(axis))])


def swap_by_core(x, even, odd):
    peers, ring = lax.axis_size("row"), lax.axis_size("loop")
    pairs = [(r * ring + l, r * ring + (l ^ (odd if r % 2 else even))) for r in range(peers) for l in range(ring)]
    return lax.ppermute(x, ("row", "loop"), pairs)


def per_device(
    features,
    weight,
    local_tiles,
    local_ids,
    local_live,
    send_rows,
    send_count,
    edge_tiles,
    edge_ids,
    edge_live,
    hub_feats,
    hub_adj,
    hub_live,
):
    peers, ring = lax.axis_size("row"), lax.axis_size("loop")
    slots = send_rows.shape[2]
    size = local_tiles.shape[1]
    tile_rows = features.shape[0] // size
    chips = range(2, peers, 2)
    near_chips = [c for c in chips if c & (c - 1) == 0]
    far_chips = [c for c in chips if c not in near_chips]
    feat, sends, counts, hub, live, *packed = pack(
        [(c, c ^ 1) for c in far_chips], features, send_rows[0], send_count, hub_feats, hub_live.T
    )
    from_far = [swap(x, "row", c) for x, c in zip(packed, far_chips)]
    packed = pack_more([(c, c ^ 1) for c in near_chips], feat, sends, counts)
    from_near = [swap(x, "row", c) for x, c in zip(packed, near_chips)]
    near = swap(hub, "loop", 1)
    far = [swap_by_core(hub, offset, offset + 1) for offset in range(2, ring, 2)]
    acc, edge_map, to_core, mask = local_term(
        feat,
        sends,
        counts,
        (local_ids, local_live, edge_ids, edge_live),
        local_tiles,
        edge_tiles,
        hub_adj,
        live,
        hub,
    )
    arrived = from_far + from_near
    shard = hub.shape[0]
    rows = [(0, slots)] + [(slots, slots)] * len(arrived) + [(0, shard)] * len(far)
    shared = swap(stack(rows, [to_core, *arrived, *far, near]), "row", 1)
    hubs = [(1, 1)] + [(2 * n + 2, 2 * n + 3) for n in range(len(far))]
    order = far_chips + near_chips
    acc = middle_term(
        hubs, order, slots, edge_map, mask, hub_adj, edge_tiles, acc, [near, *far, *arrived]
    )
    pieces = [(0, 0, 1)] + [(0, (1 + n) * slots, c ^ 1) for n, c in enumerate(order)]
    at = len(pieces) * slots
    hubs = [(0, at + n * shard, 2 * n + 3, 2 * n + 2) for n in range(len(far))]
    return last_term(pieces, hubs, slots, shard, edge_map, edge_tiles, hub_adj, mask, acc, weight, [shared])


def solution(mesh):
    both = ("row", "loop")
    placed = (
        P(both, None),
        P(),
        P(both, None, None),
        P(both),
        P(both),
        P(both, None, None),
        P(both, None),
        P(both, None, None),
        P(both),
        P(both),
        P("loop", None),
        P(both, None),
        P(both, None),
    )
    return jax.shard_map(per_device, mesh=mesh, in_specs=placed, out_specs=P(both, None), check_vma=False)
```

```python
import functools

import jax
import jax.numpy as jnp
from jax import lax
from jax.experimental import pallas as pl
from jax.experimental.pallas import tpu as pltpu
from jax.sharding import PartitionSpec as P

BF = jnp.bfloat16
F32 = jnp.float32
I32 = jnp.int32
EARLY = pl.CostEstimate(flops=1 << 35, bytes_accessed=0, transcendentals=0)
VMEM = pl.BlockSpec(memory_space=pltpu.VMEM)
SMEM = pl.BlockSpec(memory_space=pltpu.SMEM)
HBM = pl.BlockSpec(memory_space=pltpu.HBM)
ANY = pl.BlockSpec(memory_space=pl.ANY)
MIB = 1 << 20
FREE = pl.CostEstimate(flops=0, bytes_accessed=0, transcendentals=0)


def params(mib):
    return pltpu.CompilerParams(vmem_limit_bytes=mib * MIB)


def hbm(*arrays):
    return [pltpu.with_memory_space_constraint(x, pltpu.HBM) for x in arrays]


def dot(a, b):
    return jnp.dot(a, b, preferred_element_type=F32)


def picks(send_ref, count_ref, rows, peer, scalar):
    slots = send_ref.shape[1]
    index = send_ref[pl.ds(peer, 1), :]
    slot = lax.broadcasted_iota(I32, (1, slots), 1)
    if scalar:
        count = count_ref[0, peer]
    else:
        peers = lax.broadcasted_iota(I32, count_ref.shape, 1)
        count = jnp.sum(jnp.where(peers == peer, count_ref[...], 0), axis=1, keepdims=True)
    index = jnp.where(slot < count, index, -1)
    lane = lax.broadcasted_iota(I32, (128, 128), 1)
    blocks = []
    for part in range(slots // 128):
        column = jnp.broadcast_to(index[:, part * 128 : (part + 1) * 128], (128, 128)).T
        line = [jnp.where(column == lane + c * 128, 1.0, 0.0).astype(BF) for c in range(rows // 128)]
        blocks.append(jnp.concatenate(line, axis=1))
    return jnp.concatenate(blocks, axis=0)


def gather_groups(offsets, send_ref, count_ref, feat_ref, packed, scalar=False):
    me = lax.axis_index("row")
    rows = feat_ref.shape[0]
    for out_ref, group in zip(packed, offsets):
        hot = [picks(send_ref, count_ref, rows, me ^ offset, scalar) for offset in group]
        out_ref[...] = dot(jnp.concatenate(hot, axis=0), feat_ref[...]).astype(BF)


def start_all(sources, targets, sems):
    copies = [pltpu.make_async_copy(x, y, sems.at[n]) for n, (x, y) in enumerate(zip(sources, targets))]
    for copy in copies:
        copy.start()
    return copies


def wait_all(copies):
    for copy in copies:
        copy.wait()


def pack_kernel(offsets, feat_hbm, send_hbm, count_hbm, hub_hbm, live_hbm, *refs):
    targets, (*packed, scalars, sems) = refs[:5], refs[5:]
    feat_ref, send_ref = targets[:2]
    sources = [feat_hbm, send_hbm, count_hbm, hub_hbm, live_hbm, count_hbm]
    copies = start_all(sources, [*targets, scalars], sems)
    wait_all(copies[:2] + copies[5:])
    gather_groups(offsets, send_ref, scalars, feat_ref, packed, scalar=True)
    wait_all(copies[2:5])


def pack(offsets, features, send_rows, send_count, hub_feats, hub_live):
    slots, width = send_rows.shape[1], features.shape[1]
    arrays = (features, send_rows, send_count, hub_feats, hub_live)
    return pl.pallas_call(
        functools.partial(pack_kernel, offsets),
        out_shape=[jax.ShapeDtypeStruct(x.shape, x.dtype) for x in arrays]
        + [jax.ShapeDtypeStruct((len(group) * slots, width), BF) for group in offsets],
        in_specs=[HBM] * 5,
        out_specs=[VMEM] * (5 + len(offsets)),
        scratch_shapes=[pltpu.SMEM(send_count.shape, I32), pltpu.SemaphoreType.DMA((6,))],
        compiler_params=params(16),
        cost_estimate=FREE,
        name="pack",
    )(*hbm(*arrays))


def more_kernel(offsets, feat_ref, send_ref, count_ref, *packed):
    gather_groups(offsets, send_ref, count_ref, feat_ref, packed)


def pack_more(offsets, features, send_rows, send_count):
    slots, width = send_rows.shape[1], features.shape[1]
    return pl.pallas_call(
        functools.partial(more_kernel, offsets),
        out_shape=[jax.ShapeDtypeStruct((len(group) * slots, width), BF) for group in offsets],
        in_specs=[VMEM] * 3,
        out_specs=[VMEM] * len(offsets),
        compiler_params=params(16),
        cost_estimate=EARLY,
        name="more",
    )(features, send_rows, send_count)


def clear_map(map_ref):
    for cell in range(map_ref.shape[0]):
        map_ref[cell] = -1


def fill_map(ids_ref, live_ref, map_ref, first, count):
    for n in range(count):
        t = first + n
        map_ref[ids_ref[t]] = jnp.where(live_ref[t] > 0, t, -1)


def cell_tile(tiles_ref, map_ref, cell):
    slot = map_ref[cell]
    tile = tiles_ref[jnp.maximum(slot, 0)]
    return jnp.where(slot >= 0, tile, jnp.zeros_like(tile))


def edge_line(tiles_ref, map_ref, row, cols, sources, per):
    return [cell_tile(tiles_ref, map_ref, row * cols + source * per + j) for source in sources for j in range(per)]


def hub_line(adj_ref, live_ref, row, size, owner, per):
    line = []
    for b in [owner * per + j for j in range(per)]:
        cell = adj_ref[pl.ds(pl.multiple_of(row * size, size), size), pl.ds(pl.multiple_of(b * size, size), size)]
        line.append(jnp.where(live_ref[b, row] > 0, cell, jnp.zeros_like(cell)))
    return line


def local_kernel(block, feat_ref, send_ref, count_ref, tiles_ref, edge_ref, adj_ref, live_vmem, hub_ref, *refs):
    sources, (out_ref, map_hbm, core_ref, mask_ref, *refs) = refs[:4], refs[4:]
    *tables, live_ref, local_map, edge_map, rhs_ref, sems = refs
    copies = start_all([*sources, live_vmem], [*tables, live_ref], sems)
    shard = hub_ref.shape[0]
    own_ref = rhs_ref.at[shard:]
    rhs_ref[:shard, :] = hub_ref[...]
    gather_groups([(1,)], send_ref, count_ref, feat_ref, [core_ref])
    wait_all(copies)
    clear_map(local_map)
    fill_map(tables[0], tables[1], local_map, 0, tables[0].shape[0])
    clear_map(edge_map)
    gather_groups([(0,)], send_ref, count_ref, feat_ref, [own_ref])
    size = tiles_ref.shape[1]
    rows = feat_ref.shape[0]
    cols, edge_cols = rows // size, edge_map.shape[0] // (rows // size)
    steps = rows // (block * size)
    share = tables[2].shape[0] // steps

    def span(m):
        return pl.ds(pl.multiple_of(m * block * size, block * size), block * size)

    def local_body(m, _):
        blocks = []
        for i in range(block):
            row = m * block + i
            line = [cell_tile(tiles_ref, local_map, row * cols + j) for j in range(cols)]
            blocks.append(jnp.concatenate(line, axis=1))
        out_ref[span(m), :] = dot(jnp.concatenate(blocks, axis=0), feat_ref[...])
        fill_map(tables[2], tables[3], edge_map, m * share, share)
        for i in range(block):
            row = m * block + i
            hit = jnp.sum(jnp.where(at_row == row, live_vmem[...], 0), axis=1, keepdims=True)
            mask_ref[pl.ds(row, 1), :] = jnp.sum(jnp.where(inside & (hit > 0), 1.0, 0.0), axis=0, keepdims=True)
        return 0

    at_row = lax.broadcasted_iota(I32, live_vmem.shape, 1)
    cells = (live_vmem.shape[0], adj_ref.shape[1])
    lane, first = lax.broadcasted_iota(I32, cells, 1), lax.broadcasted_iota(I32, cells, 0) * size
    inside = (lane >= first) & (lane < first + size)

    lax.fori_loop(0, steps, local_body, 0)
    fill_map(tables[2], tables[3], edge_map, steps * share, tables[2].shape[0] - steps * share)
    write = pltpu.make_async_copy(edge_map, map_hbm, sems.at[5])
    write.start()
    me, loop = lax.axis_index("row"), lax.axis_index("loop")
    per = own_ref.shape[0] // size

    def own_body(m, _):
        blocks = []
        for i in range(block):
            row = m * block + i
            line = hub_line(adj_ref, live_ref, row, size, loop, shard // size)
            line += edge_line(edge_ref, edge_map, row, edge_cols, [me], per)
            blocks.append(jnp.concatenate(line, axis=1))
        out_ref[span(m), :] += dot(jnp.concatenate(blocks, axis=0), rhs_ref[...])
        return 0

    lax.fori_loop(0, steps, own_body, 0)
    write.wait()


def local_term(features, send_rows, send_count, tables, tiles, edges, adj, hub_live, hub):
    rows, width = features.shape
    peers, slots = send_rows.shape
    size = tiles.shape[1]
    local_cells, edge_cells = (rows // size) ** 2, (rows // size) * (peers * slots // size)
    return pl.pallas_call(
        functools.partial(local_kernel, 8),
        out_shape=[
            jax.ShapeDtypeStruct(features.shape, F32),
            jax.ShapeDtypeStruct((edge_cells,), I32),
            jax.ShapeDtypeStruct((slots, width), BF),
            jax.ShapeDtypeStruct((rows // size, adj.shape[1]), F32),
        ],
        in_specs=[VMEM] * 8 + [HBM] * 4,
        out_specs=[VMEM, ANY, VMEM, VMEM],
        scratch_shapes=[pltpu.SMEM(x.shape, I32) for x in tables]
        + [pltpu.SMEM(hub_live.shape, I32), pltpu.SMEM((local_cells,), I32), pltpu.SMEM((edge_cells,), I32)]
        + [pltpu.VMEM((hub.shape[0] + slots, width), BF), pltpu.SemaphoreType.DMA((6,))],
        compiler_params=params(16),
        cost_estimate=FREE,
        name="local",
    )(features, send_rows, send_count, tiles, edges, adj, hub_live, hub, *hbm(*tables))


def stack_kernel(rows, *refs):
    *array_refs, out_ref = refs
    at = 0
    for array_ref, (first, count) in zip(array_refs, rows):
        out_ref[at : at + count, :] = array_ref[first : first + count, :]
        at += count


def stack(rows, arrays):
    return pl.pallas_call(
        functools.partial(stack_kernel, rows),
        out_shape=jax.ShapeDtypeStruct((sum(count for _, count in rows), arrays[0].shape[1]), BF),
        in_specs=[VMEM] * len(arrays),
        out_specs=VMEM,
        compiler_params=params(16),
        cost_estimate=FREE,
        name="stack",
    )(*arrays)


def masked_line(adj_ref, mask_ref, row, size, columns):
    span = pl.ds(pl.multiple_of(row * size, size), size)
    line = []
    for column in columns:
        mask = jnp.broadcast_to(mask_ref[pl.ds(row, 1), column], (size, column.size)).astype(BF)
        line.append(adj_ref[span, column] * mask)
    return jnp.concatenate(line, axis=1)


def middle_kernel(block, hubs, pieces, map_ref, mask_ref, adj_ref, edge_ref, acc_ref, *refs):
    *array_refs, out_ref, edge_map, hub_rhs, rhs_ref, sem = refs
    table = pltpu.make_async_copy(map_ref, edge_map, sem)
    table.start()
    me, loop = lax.axis_index("row"), lax.axis_index("loop")
    core = lax.rem(me, 2)
    rows = mask_ref.shape[0]
    size = adj_ref.shape[0] // rows
    cols = edge_map.shape[0] // rows
    shard, slots = hub_rhs.shape[0] // len(hubs), rhs_ref.shape[0] // len(pieces)
    columns = []
    for n, (even, odd) in enumerate(hubs):
        owner = loop ^ jnp.where(core == 0, even, odd)
        columns.append(pl.ds(pl.multiple_of(owner * shard, shard), shard))
        hub_rhs[n * shard : (n + 1) * shard, :] = array_refs[n][...]
    for n in range(len(pieces)):
        rhs_ref[n * slots : (n + 1) * slots, :] = array_refs[len(hubs) + n][:slots, :]
    sources = [me ^ offset for offset in pieces]
    def span(m):
        return pl.ds(pl.multiple_of(m * block * size, block * size), block * size)

    def hub_body(m, _):
        blocks = [masked_line(adj_ref, mask_ref, m * block + i, size, columns) for i in range(block)]
        out_ref[span(m), :] = acc_ref[span(m), :] + dot(jnp.concatenate(blocks, axis=0), hub_rhs[...])
        return 0

    lax.fori_loop(0, rows // block, hub_body, 0)
    table.wait()

    lines = [edge_line(edge_ref, edge_map, row, cols, sources, slots // size) for row in range(rows)]
    found = jnp.concatenate([jnp.concatenate(line, axis=1) for line in lines], axis=0)
    out_ref[...] += dot(found, rhs_ref[...])


def middle_term(hubs, pieces, slots, edge_map, mask, adj, edges, acc, arrays):
    shard, width = arrays[0].shape
    return pl.pallas_call(
        functools.partial(middle_kernel, 8, hubs, pieces),
        out_shape=jax.ShapeDtypeStruct(acc.shape, F32),
        in_specs=[ANY] + [VMEM] * (4 + len(arrays)),
        out_specs=VMEM,
        scratch_shapes=[
            pltpu.SMEM(edge_map.shape, I32),
            pltpu.VMEM((len(hubs) * shard, width), BF),
            pltpu.VMEM((len(pieces) * slots, width), BF),
            pltpu.SemaphoreType.DMA,
        ],
        compiler_params=params(16),
        cost_estimate=FREE,
        name="middle",
    )(edge_map, mask, adj, edges, acc, *arrays)


def last_kernel(block, pieces, hubs, map_ref, edge_ref, adj_ref, mask_ref, acc_ref, weight_ref, *refs):
    *array_refs, out_ref, edge_map, hub_ref, rhs_ref, total_ref, stage_ref, sems = refs
    size = edge_ref.shape[1]
    rows = acc_ref.shape[0]
    steps = rows // (block * size)
    table = pltpu.make_async_copy(map_ref, edge_map, sems.at[steps + 1])
    table.start()
    me, loop = lax.axis_index("row"), lax.axis_index("loop")
    core = lax.rem(me, 2)
    cols = edge_map.shape[0] // (rows // size)
    slots = rhs_ref.shape[0] // len(pieces)
    shard = hub_ref.shape[0] // len(hubs)
    columns = []
    for n, (array, first, even, odd) in enumerate(hubs):
        owner = loop ^ jnp.where(core == 0, even, odd)
        columns.append(pl.ds(pl.multiple_of(owner * shard, shard), shard))
        hub_ref[n * shard : (n + 1) * shard, :] = array_refs[array][first : first + shard, :]
    for n, (array, first, _) in enumerate(pieces):
        rhs_ref[n * slots : (n + 1) * slots, :] = array_refs[array][first : first + slots, :]
    sources = [me ^ offset for _, _, offset in pieces]

    def span(m):
        return pl.ds(pl.multiple_of(m * block * size, block * size), block * size)

    def hub_body(m, _):
        blocks = [masked_line(adj_ref, mask_ref, m * block + i, size, columns) for i in range(block)]
        total_ref[span(m), :] = acc_ref[span(m), :] + dot(jnp.concatenate(blocks, axis=0), hub_ref[...])
        return 0

    lax.fori_loop(0, steps, hub_body, 0)
    table.wait()

    lines = [edge_line(edge_ref, edge_map, row, cols, sources, slots // size) for row in range(rows // size)]
    tiles = jnp.concatenate([jnp.concatenate(line, axis=1) for line in lines], axis=0)
    total_ref[...] += dot(tiles, rhs_ref[...])
    copies = []
    for n, (start, stop) in enumerate([(0, rows // 2), (rows // 2, 3 * rows // 4), (3 * rows // 4, rows)]):
        part = pl.ds(start, stop - start)
        stage_ref[part, :] = jnp.maximum(dot(total_ref[part, :].astype(BF), weight_ref[...]), 0.0).astype(BF)
        copies.append(pltpu.make_async_copy(stage_ref.at[part], out_ref.at[part], sems.at[n]))
        copies[n].start()
    wait_all(copies)


def last_term(pieces, hubs, slots, shard, edge_map, edges, adj, mask, acc, weight, arrays):
    block = 8
    rows, width = acc.shape
    return pl.pallas_call(
        functools.partial(last_kernel, block, pieces, hubs),
        out_shape=jax.ShapeDtypeStruct(acc.shape, BF),
        in_specs=[ANY] + [VMEM] * (5 + len(arrays)),
        out_specs=HBM,
        scratch_shapes=[
            pltpu.SMEM(edge_map.shape, I32),
            pltpu.VMEM((len(hubs) * shard, width), BF),
            pltpu.VMEM((len(pieces) * slots, width), BF),
            pltpu.VMEM(acc.shape, F32),
            pltpu.VMEM(acc.shape, BF),
            pltpu.SemaphoreType.DMA((rows // (block * edges.shape[1]) + 2,)),
        ],
        compiler_params=params(16),
        cost_estimate=FREE,
        name="last",
    )(edge_map, edges, adj, mask, acc, weight, *arrays)


def swap(x, axis, offset):
    return lax.ppermute(x, axis, [(i, i ^ offset) for i in range(lax.axis_size(axis))])


def swap_by_core(x, even, odd):
    peers, ring = lax.axis_size("row"), lax.axis_size("loop")
    pairs = [(r * ring + l, r * ring + (l ^ (odd if r % 2 else even))) for r in range(peers) for l in range(ring)]
    return lax.ppermute(x, ("row", "loop"), pairs)


def per_device(
    features,
    weight,
    local_tiles,
    local_ids,
    local_live,
    send_rows,
    send_count,
    edge_tiles,
    edge_ids,
    edge_live,
    hub_feats,
    hub_adj,
    hub_live,
):
    peers, ring = lax.axis_size("row"), lax.axis_size("loop")
    slots = send_rows.shape[2]
    size = local_tiles.shape[1]
    tile_rows = features.shape[0] // size
    chips = range(2, peers, 2)
    near_chips = [c for c in chips if c & (c - 1) == 0]
    far_chips = [c for c in chips if c not in near_chips]
    feat, sends, counts, hub, live, *packed = pack(
        [(c, c ^ 1) for c in far_chips], features, send_rows[0], send_count, hub_feats, hub_live.T
    )
    from_far = [swap(x, "row", c) for x, c in zip(packed, far_chips)]
    packed = pack_more([(c, c ^ 1) for c in near_chips], feat, sends, counts)
    from_near = [swap(x, "row", c) for x, c in zip(packed, near_chips)]
    near = swap(hub, "loop", 1)
    far = [swap_by_core(hub, offset, offset + 1) for offset in range(2, ring, 2)]
    acc, edge_map, to_core, mask = local_term(
        feat,
        sends,
        counts,
        (local_ids, local_live, edge_ids, edge_live),
        local_tiles,
        edge_tiles,
        hub_adj,
        live,
        hub,
    )
    arrived = from_far + from_near
    shard = hub.shape[0]
    rows = [(0, slots)] + [(slots, slots)] * len(arrived) + [(0, shard)] * len(far)
    shared = swap(stack(rows, [to_core, *arrived, *far, near]), "row", 1)
    hubs = [(1, 1)] + [(2 * n + 2, 2 * n + 3) for n in range(len(far))]
    order = far_chips + near_chips
    acc = middle_term(
        hubs, order, slots, edge_map, mask, hub_adj, edge_tiles, acc, [near, *far, *arrived]
    )
    pieces = [(0, 0, 1)] + [(0, (1 + n) * slots, c ^ 1) for n, c in enumerate(order)]
    at = len(pieces) * slots
    hubs = [(0, at + n * shard, 2 * n + 3, 2 * n + 2) for n in range(len(far))]
    return last_term(pieces, hubs, slots, shard, edge_map, edge_tiles, hub_adj, mask, acc, weight, [shared])


def solution(mesh):
    both = ("row", "loop")
    placed = (
        P(both, None),
        P(),
        P(both, None, None),
        P(both),
        P(both),
        P(both, None, None),
        P(both, None),
        P(both, None, None),
        P(both),
        P(both),
        P("loop", None),
        P(both, None),
        P(both, None),
    )
    return jax.shard_map(per_device, mesh=mesh, in_specs=placed, out_specs=P(both, None), check_vma=False)
```

```python
import functools

import jax
import jax.numpy as jnp
from jax import lax
from jax.experimental import pallas as pl
from jax.experimental.pallas import tpu as pltpu
from jax.sharding import PartitionSpec as P

BF = jnp.bfloat16
F32 = jnp.float32
I32 = jnp.int32
EARLY = pl.CostEstimate(flops=1 << 35, bytes_accessed=0, transcendentals=0)
VMEM = pl.BlockSpec(memory_space=pltpu.VMEM)
SMEM = pl.BlockSpec(memory_space=pltpu.SMEM)
HBM = pl.BlockSpec(memory_space=pltpu.HBM)
ANY = pl.BlockSpec(memory_space=pl.ANY)
MIB = 1 << 20
FREE = pl.CostEstimate(flops=0, bytes_accessed=0, transcendentals=0)


def params(mib):
    return pltpu.CompilerParams(vmem_limit_bytes=mib * MIB)


def hbm(*arrays):
    return [pltpu.with_memory_space_constraint(x, pltpu.HBM) for x in arrays]


def dot(a, b):
    return jnp.dot(a, b, preferred_element_type=F32)


def picks(send_ref, count_ref, rows, peer, scalar):
    slots = send_ref.shape[1]
    index = send_ref[pl.ds(peer, 1), :]
    slot = lax.broadcasted_iota(I32, (1, slots), 1)
    if scalar:
        count = count_ref[0, peer]
    else:
        peers = lax.broadcasted_iota(I32, count_ref.shape, 1)
        count = jnp.sum(jnp.where(peers == peer, count_ref[...], 0), axis=1, keepdims=True)
    index = jnp.where(slot < count, index, -1)
    lane = lax.broadcasted_iota(I32, (128, 128), 1)
    blocks = []
    for part in range(slots // 128):
        column = jnp.broadcast_to(index[:, part * 128 : (part + 1) * 128], (128, 128)).T
        line = [jnp.where(column == lane + c * 128, 1.0, 0.0).astype(BF) for c in range(rows // 128)]
        blocks.append(jnp.concatenate(line, axis=1))
    return jnp.concatenate(blocks, axis=0)


def gather_groups(offsets, send_ref, count_ref, feat_ref, packed, scalar=False):
    me = lax.axis_index("row")
    rows = feat_ref.shape[0]
    for out_ref, group in zip(packed, offsets):
        hot = [picks(send_ref, count_ref, rows, me ^ offset, scalar) for offset in group]
        out_ref[...] = dot(jnp.concatenate(hot, axis=0), feat_ref[...]).astype(BF)


def start_all(sources, targets, sems):
    copies = [pltpu.make_async_copy(x, y, sems.at[n]) for n, (x, y) in enumerate(zip(sources, targets))]
    for copy in copies:
        copy.start()
    return copies


def wait_all(copies):
    for copy in copies:
        copy.wait()


def pack_kernel(offsets, feat_hbm, send_hbm, count_hbm, hub_hbm, live_hbm, *refs):
    targets, (*packed, scalars, sems) = refs[:5], refs[5:]
    feat_ref, send_ref = targets[:2]
    quarter = feat_ref.shape[0] // 4
    parts = [pl.ds(n * quarter, quarter) for n in range(4)]
    sources = [send_hbm, count_hbm, *[feat_hbm.at[part] for part in parts], count_hbm, hub_hbm, live_hbm]
    copies = start_all(sources, [send_ref, scalars, *[feat_ref.at[part] for part in parts], *targets[2:]], sems)
    wait_all(copies[:6])
    gather_groups(offsets, send_ref, scalars, feat_ref, packed, scalar=True)
    wait_all(copies[6:])


def pack(offsets, features, send_rows, send_count, hub_feats, hub_live):
    slots, width = send_rows.shape[1], features.shape[1]
    arrays = (features, send_rows, send_count, hub_feats, hub_live)
    return pl.pallas_call(
        functools.partial(pack_kernel, offsets),
        out_shape=[jax.ShapeDtypeStruct(x.shape, x.dtype) for x in arrays]
        + [jax.ShapeDtypeStruct((len(group) * slots, width), BF) for group in offsets],
        in_specs=[HBM] * 5,
        out_specs=[VMEM] * (5 + len(offsets)),
        scratch_shapes=[pltpu.SMEM(send_count.shape, I32), pltpu.SemaphoreType.DMA((9,))],
        compiler_params=params(16),
        cost_estimate=FREE,
        name="pack",
    )(*hbm(*arrays))


def more_kernel(offsets, feat_ref, send_ref, count_ref, *packed):
    gather_groups(offsets, send_ref, count_ref, feat_ref, packed)


def pack_more(offsets, features, send_rows, send_count):
    slots, width = send_rows.shape[1], features.shape[1]
    return pl.pallas_call(
        functools.partial(more_kernel, offsets),
        out_shape=[jax.ShapeDtypeStruct((len(group) * slots, width), BF) for group in offsets],
        in_specs=[VMEM] * 3,
        out_specs=[VMEM] * len(offsets),
        compiler_params=params(16),
        cost_estimate=EARLY,
        name="more",
    )(features, send_rows, send_count)


def clear_map(map_ref):
    for cell in range(map_ref.shape[0]):
        map_ref[cell] = -1


def fill_map(ids_ref, live_ref, map_ref, first, count):
    for n in range(count):
        t = first + n
        map_ref[ids_ref[t]] = jnp.where(live_ref[t] > 0, t, -1)


def cell_tile(tiles_ref, map_ref, cell):
    slot = map_ref[cell]
    tile = tiles_ref[jnp.maximum(slot, 0)]
    return jnp.where(slot >= 0, tile, jnp.zeros_like(tile))


def edge_line(tiles_ref, map_ref, row, cols, sources, per):
    return [cell_tile(tiles_ref, map_ref, row * cols + source * per + j) for source in sources for j in range(per)]


def hub_line(adj_ref, live_ref, row, size, owner, per):
    line = []
    for b in [owner * per + j for j in range(per)]:
        cell = adj_ref[pl.ds(pl.multiple_of(row * size, size), size), pl.ds(pl.multiple_of(b * size, size), size)]
        line.append(jnp.where(live_ref[b, row] > 0, cell, jnp.zeros_like(cell)))
    return line


def local_kernel(block, feat_ref, send_ref, count_ref, tiles_ref, edge_ref, adj_ref, live_vmem, hub_ref, *refs):
    sources, (out_ref, map_hbm, core_ref, mask_ref, *refs) = refs[:4], refs[4:]
    *tables, live_ref, local_map, edge_map, rhs_ref, sems = refs
    copies = start_all([*sources, live_vmem], [*tables, live_ref], sems)
    shard = hub_ref.shape[0]
    own_ref = rhs_ref.at[shard:]
    rhs_ref[:shard, :] = hub_ref[...]
    gather_groups([(1,)], send_ref, count_ref, feat_ref, [core_ref])
    wait_all(copies)
    clear_map(local_map)
    fill_map(tables[0], tables[1], local_map, 0, tables[0].shape[0])
    clear_map(edge_map)
    gather_groups([(0,)], send_ref, count_ref, feat_ref, [own_ref])
    size = tiles_ref.shape[1]
    rows = feat_ref.shape[0]
    cols, edge_cols = rows // size, edge_map.shape[0] // (rows // size)
    steps = rows // (block * size)
    share = tables[2].shape[0] // steps

    def span(m):
        return pl.ds(pl.multiple_of(m * block * size, block * size), block * size)

    def local_body(m, _):
        blocks = []
        for i in range(block):
            row = m * block + i
            line = [cell_tile(tiles_ref, local_map, row * cols + j) for j in range(cols)]
            blocks.append(jnp.concatenate(line, axis=1))
        out_ref[span(m), :] = dot(jnp.concatenate(blocks, axis=0), feat_ref[...])
        fill_map(tables[2], tables[3], edge_map, m * share, share)
        for i in range(block):
            row = m * block + i
            hit = jnp.sum(jnp.where(at_row == row, live_vmem[...], 0), axis=1, keepdims=True)
            mask_ref[pl.ds(row, 1), :] = jnp.sum(jnp.where(inside & (hit > 0), 1.0, 0.0), axis=0, keepdims=True)
        return 0

    at_row = lax.broadcasted_iota(I32, live_vmem.shape, 1)
    cells = (live_vmem.shape[0], adj_ref.shape[1])
    lane, first = lax.broadcasted_iota(I32, cells, 1), lax.broadcasted_iota(I32, cells, 0) * size
    inside = (lane >= first) & (lane < first + size)

    lax.fori_loop(0, steps, local_body, 0)
    fill_map(tables[2], tables[3], edge_map, steps * share, tables[2].shape[0] - steps * share)
    write = pltpu.make_async_copy(edge_map, map_hbm, sems.at[5])
    write.start()
    me, loop = lax.axis_index("row"), lax.axis_index("loop")
    per = own_ref.shape[0] // size

    def own_body(m, _):
        blocks = []
        for i in range(block):
            row = m * block + i
            line = hub_line(adj_ref, live_ref, row, size, loop, shard // size)
            line += edge_line(edge_ref, edge_map, row, edge_cols, [me], per)
            blocks.append(jnp.concatenate(line, axis=1))
        out_ref[span(m), :] += dot(jnp.concatenate(blocks, axis=0), rhs_ref[...])
        return 0

    lax.fori_loop(0, steps, own_body, 0)
    write.wait()


def local_term(features, send_rows, send_count, tables, tiles, edges, adj, hub_live, hub):
    rows, width = features.shape
    peers, slots = send_rows.shape
    size = tiles.shape[1]
    local_cells, edge_cells = (rows // size) ** 2, (rows // size) * (peers * slots // size)
    return pl.pallas_call(
        functools.partial(local_kernel, 8),
        out_shape=[
            jax.ShapeDtypeStruct(features.shape, F32),
            jax.ShapeDtypeStruct((edge_cells,), I32),
            jax.ShapeDtypeStruct((slots, width), BF),
            jax.ShapeDtypeStruct((rows // size, adj.shape[1]), F32),
        ],
        in_specs=[VMEM] * 8 + [HBM] * 4,
        out_specs=[VMEM, ANY, VMEM, VMEM],
        scratch_shapes=[pltpu.SMEM(x.shape, I32) for x in tables]
        + [pltpu.SMEM(hub_live.shape, I32), pltpu.SMEM((local_cells,), I32), pltpu.SMEM((edge_cells,), I32)]
        + [pltpu.VMEM((hub.shape[0] + slots, width), BF), pltpu.SemaphoreType.DMA((6,))],
        compiler_params=params(16),
        cost_estimate=FREE,
        name="local",
    )(features, send_rows, send_count, tiles, edges, adj, hub_live, hub, *hbm(*tables))


def stack_kernel(rows, *refs):
    *array_refs, out_ref = refs
    at = 0
    for array_ref, (first, count) in zip(array_refs, rows):
        out_ref[at : at + count, :] = array_ref[first : first + count, :]
        at += count


def stack(rows, arrays):
    return pl.pallas_call(
        functools.partial(stack_kernel, rows),
        out_shape=jax.ShapeDtypeStruct((sum(count for _, count in rows), arrays[0].shape[1]), BF),
        in_specs=[VMEM] * len(arrays),
        out_specs=VMEM,
        compiler_params=params(16),
        cost_estimate=FREE,
        name="stack",
    )(*arrays)


def masked_line(adj_ref, mask_ref, row, size, columns):
    span = pl.ds(pl.multiple_of(row * size, size), size)
    line = []
    for column in columns:
        mask = jnp.broadcast_to(mask_ref[pl.ds(row, 1), column], (size, column.size)).astype(BF)
        line.append(adj_ref[span, column] * mask)
    return jnp.concatenate(line, axis=1)


def middle_kernel(block, hubs, pieces, map_ref, mask_ref, adj_ref, edge_ref, acc_ref, *refs):
    *array_refs, out_ref, edge_map, hub_rhs, rhs_ref, sem = refs
    table = pltpu.make_async_copy(map_ref, edge_map, sem)
    table.start()
    me, loop = lax.axis_index("row"), lax.axis_index("loop")
    core = lax.rem(me, 2)
    rows = mask_ref.shape[0]
    size = adj_ref.shape[0] // rows
    cols = edge_map.shape[0] // rows
    shard, slots = hub_rhs.shape[0] // len(hubs), rhs_ref.shape[0] // len(pieces)
    columns = []
    for n, (even, odd) in enumerate(hubs):
        owner = loop ^ jnp.where(core == 0, even, odd)
        columns.append(pl.ds(pl.multiple_of(owner * shard, shard), shard))
        hub_rhs[n * shard : (n + 1) * shard, :] = array_refs[n][...]
    for n in range(len(pieces)):
        rhs_ref[n * slots : (n + 1) * slots, :] = array_refs[len(hubs) + n][:slots, :]
    sources = [me ^ offset for offset in pieces]
    def span(m):
        return pl.ds(pl.multiple_of(m * block * size, block * size), block * size)

    def hub_body(m, _):
        blocks = [masked_line(adj_ref, mask_ref, m * block + i, size, columns) for i in range(block)]
        out_ref[span(m), :] = acc_ref[span(m), :] + dot(jnp.concatenate(blocks, axis=0), hub_rhs[...])
        return 0

    lax.fori_loop(0, rows // block, hub_body, 0)
    table.wait()

    lines = [edge_line(edge_ref, edge_map, row, cols, sources, slots // size) for row in range(rows)]
    found = jnp.concatenate([jnp.concatenate(line, axis=1) for line in lines], axis=0)
    out_ref[...] += dot(found, rhs_ref[...])


def middle_term(hubs, pieces, slots, edge_map, mask, adj, edges, acc, arrays):
    shard, width = arrays[0].shape
    return pl.pallas_call(
        functools.partial(middle_kernel, 8, hubs, pieces),
        out_shape=jax.ShapeDtypeStruct(acc.shape, F32),
        in_specs=[ANY] + [VMEM] * (4 + len(arrays)),
        out_specs=VMEM,
        scratch_shapes=[
            pltpu.SMEM(edge_map.shape, I32),
            pltpu.VMEM((len(hubs) * shard, width), BF),
            pltpu.VMEM((len(pieces) * slots, width), BF),
            pltpu.SemaphoreType.DMA,
        ],
        compiler_params=params(16),
        cost_estimate=FREE,
        name="middle",
    )(edge_map, mask, adj, edges, acc, *arrays)


def last_kernel(block, pieces, hubs, map_ref, edge_ref, adj_ref, mask_ref, acc_ref, weight_ref, *refs):
    *array_refs, out_ref, edge_map, hub_ref, rhs_ref, total_ref, stage_ref, sems = refs
    size = edge_ref.shape[1]
    rows = acc_ref.shape[0]
    steps = rows // (block * size)
    table = pltpu.make_async_copy(map_ref, edge_map, sems.at[steps + 1])
    table.start()
    me, loop = lax.axis_index("row"), lax.axis_index("loop")
    core = lax.rem(me, 2)
    cols = edge_map.shape[0] // (rows // size)
    slots = rhs_ref.shape[0] // len(pieces)
    shard = hub_ref.shape[0] // len(hubs)
    columns = []
    for n, (array, first, even, odd) in enumerate(hubs):
        owner = loop ^ jnp.where(core == 0, even, odd)
        columns.append(pl.ds(pl.multiple_of(owner * shard, shard), shard))
        hub_ref[n * shard : (n + 1) * shard, :] = array_refs[array][first : first + shard, :]
    for n, (array, first, _) in enumerate(pieces):
        rhs_ref[n * slots : (n + 1) * slots, :] = array_refs[array][first : first + slots, :]
    sources = [me ^ offset for _, _, offset in pieces]

    def span(m):
        return pl.ds(pl.multiple_of(m * block * size, block * size), block * size)

    def hub_body(m, _):
        blocks = [masked_line(adj_ref, mask_ref, m * block + i, size, columns) for i in range(block)]
        total_ref[span(m), :] = acc_ref[span(m), :] + dot(jnp.concatenate(blocks, axis=0), hub_ref[...])
        return 0

    lax.fori_loop(0, steps, hub_body, 0)
    table.wait()

    lines = [edge_line(edge_ref, edge_map, row, cols, sources, slots // size) for row in range(rows // size)]
    tiles = jnp.concatenate([jnp.concatenate(line, axis=1) for line in lines], axis=0)
    total_ref[...] += dot(tiles, rhs_ref[...])
    copies = []
    for n, (start, stop) in enumerate([(0, rows // 2), (rows // 2, 3 * rows // 4), (3 * rows // 4, rows)]):
        part = pl.ds(start, stop - start)
        stage_ref[part, :] = jnp.maximum(dot(total_ref[part, :].astype(BF), weight_ref[...]), 0.0).astype(BF)
        copies.append(pltpu.make_async_copy(stage_ref.at[part], out_ref.at[part], sems.at[n]))
        copies[n].start()
    wait_all(copies)


def last_term(pieces, hubs, slots, shard, edge_map, edges, adj, mask, acc, weight, arrays):
    block = 8
    rows, width = acc.shape
    return pl.pallas_call(
        functools.partial(last_kernel, block, pieces, hubs),
        out_shape=jax.ShapeDtypeStruct(acc.shape, BF),
        in_specs=[ANY] + [VMEM] * (5 + len(arrays)),
        out_specs=HBM,
        scratch_shapes=[
            pltpu.SMEM(edge_map.shape, I32),
            pltpu.VMEM((len(hubs) * shard, width), BF),
            pltpu.VMEM((len(pieces) * slots, width), BF),
            pltpu.VMEM(acc.shape, F32),
            pltpu.VMEM(acc.shape, BF),
            pltpu.SemaphoreType.DMA((rows // (block * edges.shape[1]) + 2,)),
        ],
        compiler_params=params(16),
        cost_estimate=FREE,
        name="last",
    )(edge_map, edges, adj, mask, acc, weight, *arrays)


def swap(x, axis, offset):
    return lax.ppermute(x, axis, [(i, i ^ offset) for i in range(lax.axis_size(axis))])


def swap_by_core(x, even, odd):
    peers, ring = lax.axis_size("row"), lax.axis_size("loop")
    pairs = [(r * ring + l, r * ring + (l ^ (odd if r % 2 else even))) for r in range(peers) for l in range(ring)]
    return lax.ppermute(x, ("row", "loop"), pairs)


def per_device(
    features,
    weight,
    local_tiles,
    local_ids,
    local_live,
    send_rows,
    send_count,
    edge_tiles,
    edge_ids,
    edge_live,
    hub_feats,
    hub_adj,
    hub_live,
):
    peers, ring = lax.axis_size("row"), lax.axis_size("loop")
    slots = send_rows.shape[2]
    size = local_tiles.shape[1]
    tile_rows = features.shape[0] // size
    chips = range(2, peers, 2)
    near_chips = [c for c in chips if c & (c - 1) == 0]
    far_chips = [c for c in chips if c not in near_chips]
    feat, sends, counts, hub, live, *packed = pack(
        [(c, c ^ 1) for c in far_chips], features, send_rows[0], send_count, hub_feats, hub_live.T
    )
    from_far = [swap(x, "row", c) for x, c in zip(packed, far_chips)]
    packed = pack_more([(c, c ^ 1) for c in near_chips], feat, sends, counts)
    from_near = [swap(x, "row", c) for x, c in zip(packed, near_chips)]
    near = swap(hub, "loop", 1)
    far = [swap_by_core(hub, offset, offset + 1) for offset in range(2, ring, 2)]
    acc, edge_map, to_core, mask = local_term(
        feat,
        sends,
        counts,
        (local_ids, local_live, edge_ids, edge_live),
        local_tiles,
        edge_tiles,
        hub_adj,
        live,
        hub,
    )
    arrived = from_far + from_near
    shard = hub.shape[0]
    rows = [(0, slots)] + [(slots, slots)] * len(arrived) + [(0, shard)] * len(far)
    shared = swap(stack(rows, [to_core, *arrived, *far, near]), "row", 1)
    hubs = [(1, 1)] + [(2 * n + 2, 2 * n + 3) for n in range(len(far))]
    order = far_chips + near_chips
    acc = middle_term(
        hubs, order, slots, edge_map, mask, hub_adj, edge_tiles, acc, [near, *far, *arrived]
    )
    pieces = [(0, 0, 1)] + [(0, (1 + n) * slots, c ^ 1) for n, c in enumerate(order)]
    at = len(pieces) * slots
    hubs = [(0, at + n * shard, 2 * n + 3, 2 * n + 2) for n in range(len(far))]
    return last_term(pieces, hubs, slots, shard, edge_map, edge_tiles, hub_adj, mask, acc, weight, [shared])


def solution(mesh):
    both = ("row", "loop")
    placed = (
        P(both, None),
        P(),
        P(both, None, None),
        P(both),
        P(both),
        P(both, None, None),
        P(both, None),
        P(both, None, None),
        P(both),
        P(both),
        P("loop", None),
        P(both, None),
        P(both, None),
    )
    return jax.shard_map(per_device, mesh=mesh, in_specs=placed, out_specs=P(both, None), check_vma=False)
```
